768 devices in a mesh: fsdp: 12 (over z), blk: 64 (over x, y, core).
Axes of the slice: x: 4, y: 8, z: 12, core: 2. Of those that a mesh axis runs over, the one named last changes fastest.
Arguments:
- grads: bfloat16 [12, 16384, 1024], P('fsdp', 'blk')
- l_codes: int32 [16384, 1024], P('blk'), may hold values from 0 to 15
- l_scales: float32 [16384, 16], P('blk'), may hold values from 0.01 to 0.12
- r_codes: int32 [16384, 1024], P('blk'), may hold values from 0 to 15
- r_scales: float32 [16384, 16], P('blk'), may hold values from 0.01 to 0.12
- l_stats: float32 [16384, 1024], P('blk'), may hold values from -3 to 3
- r_stats: float32 [16384, 1024], P('blk'), may hold values from -3 to 3
Outputs:
- update: bfloat16 [16384, 1024], P('blk')
- l_stats_new: float32 [16384, 1024], P('blk')
- r_stats_new: float32 [16384, 1024], P('blk')
The draws below stay inside these ranges and needn't reach their ends.
All inputs are finite; a program needn't handle non-finite values.
Results may differ from the reference program's by a relative error of at most 0.024.
Values may be sent and summed in bfloat16 or wider, within the bound.
A program may use at most 32 MiB of HBM per device.

```python
import math
import jax
import jax.numpy as jnp
from jax import lax

Q = 1024
NGRP = 16
BLOCKS = 16
ALLROWS = 16384
N_FSDP = 12


def draw_grads(key, part):
    key = jax.random.fold_in(key, 11)
    noise_key, row_key, column_key = jax.random.split(key, 3)
    all_rows = BLOCKS * Q
    slope_rows = 1.0 + 2.0 * (jnp.arange(all_rows) % Q).astype(jnp.float32) / Q
    row_scale = slope_rows * jnp.exp(jax.random.uniform(row_key, (all_rows,), minval=0.0, maxval=math.log(4.0)))
    column_scale = jnp.exp(jax.random.uniform(column_key, (Q,), minval=0.0, maxval=math.log(10.0)))
    noise_vals = jax.random.normal(noise_key, (N_FSDP, all_rows, Q))
    values = 0.02 * noise_vals * row_scale[None, :, None] * column_scale[None, None, :]
    return values.astype(jnp.bfloat16)


def plant(entries, rng, low, largest):
    place = [jax.random.randint(jax.random.fold_in(rng, axis), (), 0, length) for axis, length in enumerate(entries.shape)]
    widest = entries.shape.index(max(entries.shape))
    beside = place[:widest] + [(place[widest] + 1) % entries.shape[widest]] + place[widest + 1:]
    return entries.at[tuple(place)].set(low).at[tuple(beside)].set(largest)


def levels(key, extent, shards, low, top_value):
    level, own = 1.0, jax.random.fold_in(key, 6)
    for axis_at, parts in shards:
        steps = jnp.exp(jax.random.uniform(jax.random.fold_in(own, axis_at), (parts,), jnp.float32, low / len(shards), top_value / len(shards)))
        level = level * jnp.repeat(steps, extent[axis_at] // parts).reshape([-1 if axis == axis_at else 1 for axis in range(len(extent))])
    return level


def normal_values(stream_key, dims, scale, limit, shards=(), kind=jnp.bfloat16):
    gain = levels(stream_key, dims, shards, -0.22, 0.18) if shards else 1.0
    drawn = jax.random.normal(stream_key, dims, jnp.float32) * scale * gain
    return jnp.minimum(jnp.maximum(drawn, -limit), limit).astype(kind)


def setup_inputs(seed: int = 0) -> dict:
    arg_keys = jax.random.split(jax.random.key(seed), 8)
    grads = draw_grads(jax.random.fold_in(arg_keys[7], 71), 0)
    l_codes = plant(jax.random.randint(arg_keys[1], (ALLROWS, Q), 0, 16), jax.random.fold_in(arg_keys[1], 1), 0, 15).astype(jnp.int32)
    l_scales = jnp.clip(jnp.exp(math.log(0.12) - 2.4849066 * jax.random.uniform(arg_keys[2], (ALLROWS, NGRP), jnp.float32) ** levels(arg_keys[2], (ALLROWS, NGRP), ((0, 64),), -0.2, 0.2)), 0.01, 0.12)
    r_codes = plant(jax.random.randint(arg_keys[3], (ALLROWS, Q), 0, 16), jax.random.fold_in(arg_keys[3], 1), 0, 15).astype(jnp.int32)
    r_scales = jnp.clip(jnp.exp(math.log(0.12) - 2.4849066 * jax.random.uniform(arg_keys[4], (ALLROWS, NGRP), jnp.float32) ** levels(arg_keys[4], (ALLROWS, NGRP), ((0, 64),), -0.2, 0.2)), 0.01, 0.12)
    l_stats = normal_values(arg_keys[5], (ALLROWS, Q), 0.5, 3.0, ((0, 64),), jnp.float32)
    r_stats = normal_values(arg_keys[6], (ALLROWS, Q), 0.5, 3.0, ((0, 64),), jnp.float32)
    return dict(grads=grads, l_codes=l_codes, l_scales=l_scales, r_codes=r_codes, r_scales=r_scales, l_stats=l_stats, r_stats=r_stats)


BETA = 0.9
EPSILON = 1e-06

def dequantize(code_rows, scales):
    group_size = code_rows.shape[1] // scales.shape[1]
    scale_rows = jnp.repeat(scales, group_size, axis=1)
    return ((2.0 * code_rows.astype(jnp.float32) - 15.0) / 15.0 * scale_rows).astype(jnp.bfloat16)

def reference(grads, l_codes, l_scales, r_codes, r_scales, l_stats, r_stats):
    gradient = lax.optimization_barrier(jnp.sum(grads.astype(jnp.float32), axis=0)).astype(jnp.bfloat16)
    left_root = dequantize(l_codes, l_scales)
    right_root = dequantize(r_codes, r_scales)

    def per_block(block_index):
        first_row = (block_index * Q).astype(jnp.int32)
        block_grad = lax.dynamic_slice_in_dim(gradient, first_row, Q, 0)
        left_block = lax.dynamic_slice_in_dim(left_root, first_row, Q, 0)
        right_block = lax.dynamic_slice_in_dim(right_root, first_row, Q, 0)
        left_old = lax.dynamic_slice_in_dim(l_stats, first_row, Q, 0)
        right_old = lax.dynamic_slice_in_dim(r_stats, first_row, Q, 0)
        left_gram = jnp.dot(block_grad, block_grad.T, preferred_element_type=jnp.float32) / Q
        right_gram = jnp.dot(block_grad.T, block_grad, preferred_element_type=jnp.float32) / Q
        left_new = BETA * left_old + (1.0 - BETA) * left_gram
        right_new = BETA * right_old + (1.0 - BETA) * right_gram
        mixed_rows = jnp.dot(left_block, block_grad, preferred_element_type=jnp.float32).astype(jnp.bfloat16)
        product = jnp.dot(mixed_rows, right_block, preferred_element_type=jnp.float32)
        grad_mean = jnp.mean(jnp.square(block_grad.astype(jnp.float32)))
        prod_mean = jnp.mean(jnp.square(product))
        factor = jnp.sqrt(grad_mean) / jnp.sqrt(prod_mean + EPSILON)
        return ((product * factor).astype(jnp.bfloat16), left_new, right_new)
    update, left_new, right_new = lax.map(per_block, jnp.arange(BLOCKS, dtype=jnp.int32))
    return (update.reshape(BLOCKS * Q, Q), left_new.reshape(BLOCKS * Q, Q), right_new.reshape(BLOCKS * Q, Q))
```

```python
import functools

import jax
import jax.numpy as jnp
from jax import lax
from jax.experimental import pallas as pl
from jax.experimental.pallas import tpu as pltpu
from jax.sharding import PartitionSpec as P

BETA = 0.9
EPSILON = 1e-06
MESH = pl.DeviceIdType.MESH
F32 = jnp.float32
BF16 = jnp.bfloat16

ROWS = 256
ORDER = 1024
TEAM = 4
RING = 12
LANES = 128
CHUNK = 176
GROUP = 3 * CHUNK
PANEL_ROWS = RING * CHUNK
PAIRS = 4

KEYS = (-5, -4, -3, -2, -1, 1, 2, 3, 4, 5, 6)
SLOT = {key: at for at, key in enumerate(KEYS)}
SLOT[0] = 11
RS = {name: at for at, name in enumerate(
    [("a", 1), ("a", -1), ("b", 1), ("c", 1), ("c", -1), ("d", 1), ("d", -1),
     ("e", 1), ("e", -1), ("f", 1), ("f", -1)])}


def panel_row(pair, half):
    return pair * GROUP + half * ROWS


def kernel(grads, l_codes, l_scales, r_codes, r_scales, l_stats, r_stats,
           update, l_out, r_out,
           x, acc, rbuf, gall, l_code_v, r_code_v, l_scale_v, r_scale_v, l_stat_v, r_stat_v,
           l_root, r_all, mixed, prod, upd_v, sq,
           load_sem, rs_send, rs_recv, ag_send, ag_recv, y_send, y_recv, c_send, c_recv,
           r_send, r_recv, s_send, s_recv, out_sem):
    z = lax.axis_index("fsdp")
    blk = lax.axis_index("blk")
    member = lax.rem(blk, TEAM)
    base = blk - member
    m_y = lax.rem(member + 2, TEAM)
    m_c = member + 1 - 2 * lax.rem(member, 2)
    m_yc = lax.rem(m_c + 2, TEAM)

    def ring(step):
        return (lax.rem(z + step + RING, RING), blk)

    def mate(which):
        return (z, base + which)

    grad_loads = []
    for panel in range(2 * PAIRS):
        grad_loads.append(pltpu.make_async_copy(
            grads.at[0, :, pl.ds(panel * LANES, LANES)],
            x.at[pl.ds(panel_row(panel // 2, panel % 2), ROWS)], load_sem.at[panel]))
    other = [
        pltpu.make_async_copy(r_scales, r_scale_v, load_sem.at[8]),
        pltpu.make_async_copy(r_codes, r_code_v, load_sem.at[9]),
        pltpu.make_async_copy(l_scales, l_scale_v, load_sem.at[10]),
        pltpu.make_async_copy(l_codes, l_code_v, load_sem.at[11]),
        pltpu.make_async_copy(l_stats, l_stat_v, load_sem.at[12]),
        pltpu.make_async_copy(r_stats, r_stat_v, load_sem.at[13]),
    ]
    for copy in grad_loads + other:
        copy.start()

    barrier = pltpu.get_barrier_semaphore()
    partners = [ring(1), ring(-1), ring(2), ring(-2), mate(m_y), mate(m_c), mate(m_yc)]
    for partner in partners:
        pl.semaphore_signal(barrier, inc=1, device_id=partner, device_id_type=MESH)
    for pair in range(PAIRS):
        x[pl.ds(pair * GROUP + 2 * ROWS, 16), :] = jnp.zeros((16, LANES), BF16)
    pl.semaphore_wait(barrier, len(partners))

    def chunk_at(key):
        owner = lax.rem(z + key + RING, RING)
        return pl.ds(pl.multiple_of(owner * CHUNK, 16), CHUNK)

    def remote(src, dst, send, recv, target):
        return pltpu.make_async_remote_copy(
            src_ref=src, dst_ref=dst, send_sem=send, recv_sem=recv,
            device_id=target, device_id_type=MESH)

    sends = []

    def rs_copy(src, name, step):
        copy = remote(src, rbuf.at[RS[name]], rs_send.at[RS[name]], rs_recv.at[RS[name]], ring(step))
        copy.start()
        sends.append(copy)

    def rs_wait(name):
        at = RS[name]
        remote(rbuf.at[at], rbuf.at[at], rs_send.at[at], rs_recv.at[at], ring(1)).wait_recv()
        return rbuf[at].astype(F32)

    for copy in grad_loads:
        copy.wait()
    rs_copy(x.at[chunk_at(6)], ("b", 1), 2)
    rs_copy(x.at[chunk_at(-5)], ("a", -1), -1)
    rs_copy(x.at[chunk_at(5)], ("a", 1), 1)
    for s in (1, -1):
        rs_copy(x.at[chunk_at(3 * s)], ("c", s), s)
    for s in (1, -1):
        rs_copy(x.at[chunk_at(s)], ("e", s), s)

    spread_group = lax.broadcasted_iota(jnp.int32, (48, ORDER), 0) % 16
    spread_column = lax.broadcasted_iota(jnp.int32, (48, ORDER), 1) // 64
    spread = jnp.where(spread_group == spread_column, 1.0, 0.0).astype(BF16)

    def dequantize(codes, scales):
        scaled = scales[...] * (1.0 / 15.0)
        first = scaled.astype(BF16)
        rest = scaled - first.astype(F32)
        second = rest.astype(BF16)
        third = (rest - second.astype(F32)).astype(BF16)
        terms = jnp.concatenate([first.astype(F32), second.astype(F32), third.astype(F32)], axis=0)
        wide = lax.dot_general(jnp.transpose(terms).astype(BF16), spread, (((1,), (0,)), ((), ())),
                               preferred_element_type=F32)
        return ((2.0 * codes[...].astype(F32) - 15.0) * wide).astype(BF16)

    for copy in other[:2]:
        copy.wait()
    r_all[member] = dequantize(r_code_v, r_scale_v)
    r_y = remote(r_all.at[member], r_all.at[member], r_send.at[0], r_recv.at[0], mate(m_y))
    r_c = remote(r_all.at[member], r_all.at[member], r_send.at[1], r_recv.at[1], mate(m_c))
    r_y.start()
    r_c.start()

    for s in (-1, 1):
        total = x[chunk_at(4 * s), :].astype(F32) + rs_wait(("a", s))
        if s == 1:
            total = total + rs_wait(("b", 1))
        acc[0 if s == 1 else 1] = total.astype(BF16)
        rs_copy(acc.at[0 if s == 1 else 1], ("d", s), 2 * s)
    for copy in other[2:4]:
        copy.wait()
    l_root[...] = dequantize(l_code_v, l_scale_v)
    for s in (-1, 1):
        total = x[chunk_at(2 * s), :].astype(F32) + rs_wait(("c", s)) + rs_wait(("d", s))
        acc[2 if s == 1 else 3] = total.astype(BF16)
        rs_copy(acc.at[2 if s == 1 else 3], ("f", s), 2 * s)
    total = x[chunk_at(0), :].astype(F32)
    for s in (-1, 1):
        total = total + rs_wait(("e", s)) + rs_wait(("f", s))
    gall[member, chunk_at(0), :] = total.astype(BF16)

    def z_send(key, step):
        to = key - step
        at = SLOT[6 if to == -6 else to]
        ref = gall.at[member, chunk_at(key)]
        copy = remote(ref, ref, ag_send.at[at], ag_recv.at[at], ring(step))
        copy.start()
        sends.append(copy)

    def z_wait(key):
        ref = gall.at[member, chunk_at(key)]
        at = SLOT[key]
        remote(ref, ref, ag_send.at[at], ag_recv.at[at], ring(1)).wait_recv()

    def y_forward(key):
        ref = gall.at[member, chunk_at(key)]
        at = SLOT[key]
        copy = remote(ref, ref, y_send.at[at], y_recv.at[at], mate(m_y))
        copy.start()
        sends.append(copy)

    def c_forward(key, which, set_at):
        ref = gall.at[which, chunk_at(key)]
        at = SLOT[key] + 12 * set_at
        copy = remote(ref, ref, c_send.at[at], c_recv.at[at], mate(m_c))
        copy.start()
        sends.append(copy)

    def y_wait(key):
        ref = gall.at[m_y, chunk_at(key)]
        at = SLOT[key]
        remote(ref, ref, y_send.at[at], y_recv.at[at], mate(m_y)).wait_recv()
        c_forward(key, m_y, 1)

    def c_wait(key, which, set_at):
        ref = gall.at[which, chunk_at(key)]
        at = SLOT[key] + 12 * set_at
        remote(ref, ref, c_send.at[at], c_recv.at[at], mate(m_c)).wait_recv()

    for s in (1, -1):
        z_send(0, 2 * s)
    for s in (1, -1):
        z_send(0, s)
    y_forward(0)
    c_forward(0, member, 0)
    remote(r_all.at[m_y], r_all.at[m_y], r_send.at[0], r_recv.at[0], mate(m_y)).wait_recv()
    r_yc = remote(r_all.at[m_y], r_all.at[m_y], r_send.at[2], r_recv.at[2], mate(m_c))
    r_yc.start()
    for s in (1, -1):
        z_wait(-2 * s)
        z_send(-2 * s, 2 * s)
        z_send(-2 * s, s)
        y_forward(-2 * s)
        c_forward(-2 * s, member, 0)
    for s in (1, -1):
        z_wait(-s)
        y_forward(-s)
        c_forward(-s, member, 0)
    y_wait(0)
    for s in (1, -1):
        z_wait(-4 * s)
        if s == 1:
            z_send(-4, 2)
        z_send(-4 * s, s)
        y_forward(-4 * s)
        c_forward(-4 * s, member, 0)
    for s in (1, -1):
        z_wait(-3 * s)
        y_forward(-3 * s)
        c_forward(-3 * s, member, 0)
    for key in (-2, 2, -1, 1):
        y_wait(key)
    for key in (-5, 5, 6):
        z_wait(key)
        y_forward(key)
        c_forward(key, member, 0)
    for key in (-4, 4, -3, 3, -5, 5, 6):
        y_wait(key)
    remote(r_all.at[m_c], r_all.at[m_c], r_send.at[1], r_recv.at[1], mate(m_c)).wait_recv()
    remote(r_all.at[m_yc], r_all.at[m_yc], r_send.at[2], r_recv.at[2], mate(m_c)).wait_recv()
    for key in (0,) + KEYS:
        c_wait(key, m_c, 0)
    for key in (0,) + KEYS:
        c_wait(key, m_yc, 1)

    def columns(pair):
        parts = []
        for which in range(TEAM):
            parts.append(jnp.concatenate(
                [gall[which, pl.ds(panel_row(pair, half), ROWS), :] for half in (0, 1)], axis=1))
        return jnp.concatenate(parts, axis=0)

    def rows_of(which):
        return jnp.concatenate(
            [gall[which, pl.ds(panel_row(panel // 2, panel % 2), ROWS), :]
             for panel in range(2 * PAIRS)], axis=1)

    for pair in range(PAIRS):
        mixed[:, pl.ds(pair * ROWS, ROWS)] = jnp.dot(
            l_root[...], columns(pair), preferred_element_type=F32).astype(BF16)
    square = jnp.zeros((ROWS, ROWS), F32)
    for pair in range(PAIRS):
        right = jnp.concatenate([r_all[which, :, pl.ds(pair * ROWS, ROWS)] for which in range(TEAM)], axis=0)
        part = jnp.dot(mixed[...], right, preferred_element_type=F32)
        prod[:, pl.ds(pair * ROWS, ROWS)] = part
        square = square + part * part
    mine = rows_of(member)
    grad_square = jnp.sum(jnp.square(mine.astype(F32)), axis=0, keepdims=True)
    grad_square = sum(grad_square[:, at * LANES:(at + 1) * LANES] for at in range(8))
    prod_square = jnp.sum(square, axis=0, keepdims=True)
    prod_square = prod_square[:, :LANES] + prod_square[:, LANES:]
    sq[3] = jnp.concatenate(
        [jnp.broadcast_to(grad_square, (8, LANES)), jnp.broadcast_to(prod_square, (8, LANES))], axis=0)
    for at, which in enumerate((m_y, m_c, m_yc)):
        copy = remote(sq.at[3], sq.at[at], s_send.at[at], s_recv.at[at], mate(which))
        copy.start()
        sends.append(copy)

    for copy in other[4:]:
        copy.wait()
    scale = (1.0 - BETA) / ORDER
    for which in range(TEAM):
        cut = pl.ds(which * ROWS, ROWS)
        gram = lax.dot_general(mine, rows_of(which), (((1,), (1,)), ((), ())), preferred_element_type=F32)
        l_stat_v[:, cut] = BETA * l_stat_v[:, cut] + scale * gram
    l_store = pltpu.make_async_copy(l_stat_v, l_out, out_sem.at[0])
    l_store.start()
    own_columns = []
    for which in range(TEAM):
        halves = []
        for half in (0, 1):
            start = pl.multiple_of(member * GROUP + half * ROWS, 16)
            halves.append(gall[which, pl.ds(start, ROWS), :])
        own_columns.append(jnp.transpose(jnp.concatenate(halves, axis=1)))
    own_columns = jnp.concatenate(own_columns, axis=1)
    for pair in range(PAIRS):
        cut = pl.ds(pair * ROWS, ROWS)
        gram = jnp.dot(own_columns, columns(pair), preferred_element_type=F32)
        r_stat_v[:, cut] = BETA * r_stat_v[:, cut] + scale * gram
    r_store = pltpu.make_async_copy(r_stat_v, r_out, out_sem.at[1])
    r_store.start()

    for at in range(3):
        remote(sq.at[at], sq.at[at], s_send.at[at], s_recv.at[at], mate(m_y)).wait_recv()
    both = sq[0] + sq[1] + sq[2] + sq[3]
    entries = float(ORDER * ORDER)
    grad_mean = jnp.sum(both[0:1, :], axis=1, keepdims=True) / entries
    prod_mean = jnp.sum(both[8:9, :], axis=1, keepdims=True) / entries
    factor = jnp.sqrt(grad_mean) / jnp.sqrt(prod_mean + EPSILON)
    upd_v[...] = (prod[...] * factor).astype(BF16)
    u_store = pltpu.make_async_copy(upd_v, update, out_sem.at[2])
    u_store.start()
    for copy in sends + [r_y, r_c, r_yc]:
        copy.wait_send()
    l_store.wait()
    r_store.wait()
    u_store.wait()


def shards(grads, l_codes, l_scales, r_codes, r_scales, l_stats, r_stats):
    any_spec = pl.BlockSpec(memory_space=pl.ANY)
    wide = (ROWS, ORDER)
    dma = pltpu.SemaphoreType.DMA
    return pl.pallas_call(
        kernel,
        name="shampoo",
        out_shape=(
            jax.ShapeDtypeStruct(wide, BF16),
            jax.ShapeDtypeStruct(wide, F32),
            jax.ShapeDtypeStruct(wide, F32),
        ),
        in_specs=[any_spec] * 7,
        out_specs=(any_spec,) * 3,
        scratch_shapes=[
            pltpu.VMEM((PANEL_ROWS, LANES), BF16),
            pltpu.VMEM((4, CHUNK, LANES), BF16),
            pltpu.VMEM((11, CHUNK, LANES), BF16),
            pltpu.VMEM((TEAM, PANEL_ROWS, LANES), BF16),
            pltpu.VMEM(wide, jnp.int32),
            pltpu.VMEM(wide, jnp.int32),
            pltpu.VMEM((16, ROWS), F32),
            pltpu.VMEM((16, ROWS), F32),
            pltpu.VMEM(wide, F32),
            pltpu.VMEM(wide, F32),
            pltpu.VMEM(wide, BF16),
            pltpu.VMEM((TEAM, ROWS, ORDER), BF16),
            pltpu.VMEM(wide, BF16),
            pltpu.VMEM(wide, F32),
            pltpu.VMEM(wide, BF16),
            pltpu.VMEM((4, 16, LANES), F32),
            dma((14,)), dma((11,)), dma((11,)), dma((12,)), dma((12,)), dma((12,)), dma((12,)),
            dma((24,)), dma((24,)), dma((3,)), dma((3,)), dma((3,)), dma((3,)), dma((3,)),
        ],
        compiler_params=pltpu.CompilerParams(
            collective_id=0, has_side_effects=True, vmem_limit_bytes=63 * 2**20),
    )(grads, l_codes, l_scales.T, r_codes, r_scales.T, l_stats, r_stats)


def solution(mesh):
    return jax.shard_map(
        shards,
        mesh=mesh,
        in_specs=(
            P("fsdp", "blk", None),
            P("blk", None),
            P("blk", None),
            P("blk", None),
            P("blk", None),
            P("blk", None),
            P("blk", None),
        ),
        out_specs=(P("blk", None), P("blk", None), P("blk", None)),
        check_vma=False,
    )
```

```python
import functools

import jax
import jax.numpy as jnp
from jax import lax
from jax.experimental import pallas as pl
from jax.experimental.pallas import tpu as pltpu
from jax.sharding import PartitionSpec as P

BETA = 0.9
EPSILON = 1e-06
MESH = pl.DeviceIdType.MESH
F32 = jnp.float32
BF16 = jnp.bfloat16

ROWS = 256
ORDER = 1024
TEAM = 4
RING = 12
LANES = 128
CHUNK = 176
GROUP = 3 * CHUNK
PAIRS = 4

KEYS = (0, -3, 3, -1, 1, -4, 4, -2, 2, -5, 5, 6)
SLOT = {key: at for at, key in enumerate(KEYS)}
LEAVES = (("far", 1), ("two", 1), ("two", -1), ("one", 1), ("one", -1), ("back", 1), ("back", -1))
RS = {name: at for at, name in enumerate(
    LEAVES + (("near", 1), ("near", -1), ("node", 1), ("node", -1)))}
PIECES = ((0, 96), (96, 80))


def kernel(grads, l_codes, l_scales, r_codes, r_scales, l_stats, r_stats,
           update, l_out, r_out,
           x, acc, rbuf, gall, l_code_v, r_code_v, l_scale_v, r_scale_v,
           l_root, r_all, mixed, prod, sq,
           load_sem, rs_send, rs_recv, ag_send, ag_recv, y_send, y_recv, c_send, c_recv,
           r_send, r_recv, s_send, s_recv):
    z = lax.axis_index("fsdp")
    blk = lax.axis_index("blk")
    member = lax.rem(blk, TEAM)
    base = blk - member
    m_y = lax.rem(member + 2, TEAM)
    m_c = member + 1 - 2 * lax.rem(member, 2)
    m_yc = lax.rem(m_c + 2, TEAM)

    def ring(step):
        return (lax.rem(z + step + RING, RING), blk)

    def mate(which):
        return (z, base + which)

    grad_loads = []
    for pair in range(PAIRS):
        for panel, row, rows, chunk, at in (
                (0, 0, 176, 0, 0), (0, 176, 80, 1, 0), (1, 0, 96, 1, 80), (1, 96, 160, 2, 0)):
            grad_loads.append(pltpu.make_async_copy(
                grads.at[0, pl.ds(row, rows), pl.ds((2 * pair + panel) * LANES, LANES)],
                x.at[3 * pair + chunk, pl.ds(at, rows)], load_sem.at[len(grad_loads)]))
    other = [
        pltpu.make_async_copy(r_scales, r_scale_v, load_sem.at[16]),
        pltpu.make_async_copy(r_codes, r_code_v, load_sem.at[17]),
        pltpu.make_async_copy(l_scales, l_scale_v, load_sem.at[18]),
        pltpu.make_async_copy(l_codes, l_code_v, load_sem.at[19]),
        pltpu.make_async_copy(l_stats, l_out, load_sem.at[20]),
        pltpu.make_async_copy(r_stats, r_out, load_sem.at[21]),
    ]
    for copy in grad_loads + other:
        copy.start()

    barrier = pltpu.get_barrier_semaphore()
    partners = [ring(step) for step in (3, -3, 2, -2, 1, -1)] + [mate(m_y), mate(m_c), mate(m_yc)]
    for partner in partners:
        pl.semaphore_signal(barrier, inc=1, device_id=partner, device_id_type=MESH)
    for pair in range(PAIRS):
        x[3 * pair + 2, pl.ds(160, 16), :] = jnp.zeros((16, LANES), BF16)
    pl.semaphore_wait(barrier, len(partners))

    def owner(key):
        return lax.rem(z + key + RING, RING)

    def remote(src, dst, send, recv, target):
        return pltpu.make_async_remote_copy(
            src_ref=src, dst_ref=dst, send_sem=send, recv_sem=recv,
            device_id=target, device_id_type=MESH)

    sends = []

    def rs_copy(src, name, piece, step):
        at = piece * 11 + RS[name]
        cut = pl.ds(*PIECES[piece])
        copy = remote(src, rbuf.at[RS[name], cut], rs_send.at[at], rs_recv.at[at], ring(step))
        copy.start()
        sends.append(copy)

    def rs_wait(name, piece):
        at = piece * 11 + RS[name]
        ref = rbuf.at[RS[name], pl.ds(*PIECES[piece])]
        remote(ref, ref, rs_send.at[at], rs_recv.at[at], ring(1)).wait_recv()
        return ref[...].astype(F32)

    def turn(piece):
        return 1 if piece % 2 == 0 else -1

    for copy in grad_loads:
        copy.wait()
    for piece in range(len(PIECES)):
        cut = pl.ds(*PIECES[piece])
        s = turn(piece)
        rs_copy(x.at[owner(6), cut], ("far", 1), piece, 3 * s)
        for s in (1, -1):
            rs_copy(x.at[owner(5 * s), cut], ("two", s), piece, 2 * s)
        for s in (1, -1):
            rs_copy(x.at[owner(4 * s), cut], ("one", s), piece, s)
        for s in (1, -1):
            rs_copy(x.at[owner(2 * s), cut], ("back", s), piece, -s)

    spread_group = lax.broadcasted_iota(jnp.int32, (48, ORDER), 0) % 16
    spread_column = lax.broadcasted_iota(jnp.int32, (48, ORDER), 1) // 64
    spread = jnp.where(spread_group == spread_column, 1.0, 0.0).astype(BF16)

    def dequantize(codes, scales):
        scaled = scales[...] * (1.0 / 15.0)
        first = scaled.astype(BF16)
        rest = scaled - first.astype(F32)
        second = rest.astype(BF16)
        third = (rest - second.astype(F32)).astype(BF16)
        terms = jnp.concatenate([first.astype(F32), second.astype(F32), third.astype(F32)], axis=0)
        wide = lax.dot_general(jnp.transpose(terms).astype(BF16), spread, (((1,), (0,)), ((), ())),
                               preferred_element_type=F32)
        return ((2.0 * codes[...].astype(F32) - 15.0) * wide).astype(BF16)

    for copy in other[:2]:
        copy.wait()
    r_all[member] = dequantize(r_code_v, r_scale_v)
    r_y = remote(r_all.at[member], r_all.at[member], r_send.at[0], r_recv.at[0], mate(m_y))
    r_c = remote(r_all.at[member], r_all.at[member], r_send.at[1], r_recv.at[1], mate(m_c))
    r_y.start()
    r_c.start()

    for piece in range(len(PIECES)):
        cut = pl.ds(*PIECES[piece])
        for s in (-turn(piece), turn(piece)):
            total = x[owner(3 * s), cut, :].astype(F32)
            for name in ("one", "back", "two"):
                total = total + rs_wait((name, s), piece)
            if s == turn(piece):
                total = total + rs_wait(("far", 1), piece)
            at = 0 if s == 1 else 1
            acc[at, cut, :] = total.astype(BF16)
            rs_copy(acc.at[at, cut], ("node", s), piece, 3 * s)
        for s in (1, -1):
            rs_copy(x.at[owner(s), cut], ("near", s), piece, s)
    for copy in other[2:4]:
        copy.wait()
    l_root[...] = dequantize(l_code_v, l_scale_v)

    def z_send(key, piece, step):
        to = key - step
        at = piece * 12 + SLOT[6 if to == -6 else to]
        ref = gall.at[member, owner(key), pl.ds(*PIECES[piece])]
        copy = remote(ref, ref, ag_send.at[at], ag_recv.at[at], ring(step))
        copy.start()
        sends.append(copy)

    def z_wait(key, piece):
        at = piece * 12 + SLOT[key]
        ref = gall.at[member, owner(key), pl.ds(*PIECES[piece])]
        remote(ref, ref, ag_send.at[at], ag_recv.at[at], ring(1)).wait_recv()

    def y_forward(key, piece):
        at = piece * 12 + SLOT[key]
        ref = gall.at[member, owner(key), pl.ds(*PIECES[piece])]
        copy = remote(ref, ref, y_send.at[at], y_recv.at[at], mate(m_y))
        copy.start()
        sends.append(copy)

    def y_wait(key, piece):
        at = piece * 12 + SLOT[key]
        ref = gall.at[m_y, owner(key), pl.ds(*PIECES[piece])]
        remote(ref, ref, y_send.at[at], y_recv.at[at], mate(m_y)).wait_recv()

    def c_copy(which, piece, set_at):
        at = piece * 2 + set_at
        ref = gall.at[which, :, pl.ds(*PIECES[piece])]
        return remote(ref, ref, c_send.at[at], c_recv.at[at], mate(m_c))

    def c_forward(which, piece, set_at):
        copy = c_copy(which, piece, set_at)
        copy.start()
        sends.append(copy)

    for piece in range(len(PIECES)):
        cut = pl.ds(*PIECES[piece])
        total = x[z, cut, :].astype(F32)
        for name in ("near", "node"):
            for s in (-turn(piece), turn(piece)):
                total = total + rs_wait((name, s), piece)
        gall[member, z, cut, :] = total.astype(BF16)
        for s in (turn(piece), -turn(piece)):
            z_send(0, piece, 3 * s)
        for s in (1, -1):
            z_send(0, piece, s)
        y_forward(0, piece)
    for piece in range(len(PIECES)):
        for s in (turn(piece), -turn(piece)):
            z_wait(-3 * s, piece)
            if s == turn(piece):
                z_send(-3 * s, piece, 3 * s)
            z_send(-3 * s, piece, 2 * s)
            z_send(-3 * s, piece, s)
            z_send(-3 * s, piece, -s)
            y_forward(-3 * s, piece)
        for s in (1, -1):
            z_wait(-s, piece)
            y_forward(-s, piece)
    remote(r_all.at[m_y], r_all.at[m_y], r_send.at[0], r_recv.at[0], mate(m_y)).wait_recv()
    r_yc = remote(r_all.at[m_y], r_all.at[m_y], r_send.at[2], r_recv.at[2], mate(m_c))
    r_yc.start()
    for piece in range(len(PIECES)):
        for key in KEYS[5:]:
            z_wait(key, piece)
            y_forward(key, piece)
        c_forward(member, piece, 0)
    for piece in range(len(PIECES)):
        for key in KEYS:
            y_wait(key, piece)
        c_forward(m_y, piece, 1)
    remote(r_all.at[m_c], r_all.at[m_c], r_send.at[1], r_recv.at[1], mate(m_c)).wait_recv()
    remote(r_all.at[m_yc], r_all.at[m_yc], r_send.at[2], r_recv.at[2], mate(m_c)).wait_recv()
    for piece in range(len(PIECES)):
        c_copy(m_c, piece, 0).wait_recv()
        c_copy(m_yc, piece, 1).wait_recv()

    def panel_pair(which, pair):
        both = gall[which, pl.ds(3 * pair, 3)].reshape(GROUP, LANES)
        return jnp.concatenate([both[:ROWS], both[ROWS:2 * ROWS]], axis=1)

    def columns(pair):
        parts = []
        for which in range(TEAM):
            parts.append(panel_pair(which, pair))
        return jnp.concatenate(parts, axis=0)

    def rows_of(which):
        return jnp.concatenate([panel_pair(which, pair) for pair in range(PAIRS)], axis=1)

    for pair in range(PAIRS):
        mixed[:, pl.ds(pair * ROWS, ROWS)] = jnp.dot(
            l_root[...], columns(pair), preferred_element_type=F32).astype(BF16)
    square = jnp.zeros((ROWS, ROWS), F32)
    for pair in range(PAIRS):
        right = jnp.concatenate([r_all[which, :, pl.ds(pair * ROWS, ROWS)] for which in range(TEAM)], axis=0)
        part = jnp.dot(mixed[...], right, preferred_element_type=F32)
        prod[:, pl.ds(pair * ROWS, ROWS)] = part
        square = square + part * part
    mine = rows_of(member)
    grad_square = jnp.sum(jnp.square(mine.astype(F32)), axis=0, keepdims=True)
    grad_square = sum(grad_square[:, at * LANES:(at + 1) * LANES] for at in range(8))
    prod_square = jnp.sum(square, axis=0, keepdims=True)
    prod_square = prod_square[:, :LANES] + prod_square[:, LANES:]
    sq[3] = jnp.concatenate(
        [jnp.broadcast_to(grad_square, (8, LANES)), jnp.broadcast_to(prod_square, (8, LANES))], axis=0)
    for at, which in enumerate((m_y, m_c, m_yc)):
        copy = remote(sq.at[3], sq.at[at], s_send.at[at], s_recv.at[at], mate(which))
        copy.start()
        sends.append(copy)

    for copy in other[4:]:
        copy.wait()
    scale = (1.0 - BETA) / ORDER
    for which in range(TEAM):
        cut = pl.ds(which * ROWS, ROWS)
        gram = lax.dot_general(mine, rows_of(which), (((1,), (1,)), ((), ())), preferred_element_type=F32)
        l_out[:, cut] = BETA * l_out[:, cut] + scale * gram
    own_columns = []
    for which in range(TEAM):
        own_columns.append(jnp.transpose(panel_pair(which, member)))
    own_columns = jnp.concatenate(own_columns, axis=1)
    for pair in range(PAIRS):
        cut = pl.ds(pair * ROWS, ROWS)
        gram = jnp.dot(own_columns, columns(pair), preferred_element_type=F32)
        r_out[:, cut] = BETA * r_out[:, cut] + scale * gram

    for at in range(3):
        remote(sq.at[at], sq.at[at], s_send.at[at], s_recv.at[at], mate(m_y)).wait_recv()
    both = sq[0] + sq[1] + sq[2] + sq[3]
    entries = float(ORDER * ORDER)
    grad_mean = jnp.sum(both[0:1, :], axis=1, keepdims=True) / entries
    prod_mean = jnp.sum(both[8:9, :], axis=1, keepdims=True) / entries
    factor = jnp.sqrt(grad_mean) / jnp.sqrt(prod_mean + EPSILON)
    update[...] = (prod[...] * factor).astype(BF16)
    for copy in sends + [r_y, r_c, r_yc]:
        copy.wait_send()


def store_kernel(a, b, c, a_out, b_out, c_out, sem):
    copies = []
    for src, dst in ((b, b_out), (c, c_out), (a, a_out)):
        for part in range(4):
            cut = pl.ds(part * 64, 64)
            copies.append(pltpu.make_async_copy(src.at[cut], dst.at[cut], sem.at[len(copies)]))
    for copy in copies:
        copy.start()
    for copy in copies:
        copy.wait()


def shards(grads, l_codes, l_scales, r_codes, r_scales, l_stats, r_stats):
    any_spec = pl.BlockSpec(memory_space=pl.ANY)
    wide = (ROWS, ORDER)
    dma = pltpu.SemaphoreType.DMA
    pieces = len(PIECES)
    outs = pl.pallas_call(
        kernel,
        name="shampoo",
        out_shape=(
            pltpu.VMEM(wide, BF16),
            pltpu.VMEM(wide, F32),
            pltpu.VMEM(wide, F32),
        ),
        in_specs=[any_spec] * 7,
        out_specs=(pl.BlockSpec(memory_space=pltpu.VMEM),) * 3,
        scratch_shapes=[
            pltpu.VMEM((RING, CHUNK, LANES), BF16),
            pltpu.VMEM((2, CHUNK, LANES), BF16),
            pltpu.VMEM((11, CHUNK, LANES), BF16),
            pltpu.VMEM((TEAM, RING, CHUNK, LANES), BF16),
            pltpu.VMEM(wide, jnp.int32),
            pltpu.VMEM(wide, jnp.int32),
            pltpu.VMEM((16, ROWS), F32),
            pltpu.VMEM((16, ROWS), F32),
            pltpu.VMEM(wide, BF16),
            pltpu.VMEM((TEAM, ROWS, ORDER), BF16),
            pltpu.VMEM(wide, BF16),
            pltpu.VMEM(wide, F32),
            pltpu.VMEM((4, 16, LANES), F32),
            dma((22,)), dma((11 * pieces,)), dma((11 * pieces,)), dma((12 * pieces,)), dma((12 * pieces,)),
            dma((12 * pieces,)), dma((12 * pieces,)), dma((2 * pieces,)), dma((2 * pieces,)),
            dma((3,)), dma((3,)), dma((3,)), dma((3,)),
        ],
        compiler_params=pltpu.CompilerParams(
            collective_id=0, has_side_effects=True, vmem_limit_bytes=40 * 2**20),
    )(*[pltpu.with_memory_space_constraint(a, pltpu.HBM) for a in (grads, l_codes, l_scales.T, r_codes, r_scales.T, l_stats, r_stats)])
    return pl.pallas_call(
        store_kernel,
        name="store",
        out_shape=(pltpu.HBM(wide, BF16), pltpu.HBM(wide, F32), pltpu.HBM(wide, F32)),
        in_specs=[any_spec] * 3,
        out_specs=(any_spec,) * 3,
        scratch_shapes=[dma((12,))],
        compiler_params=pltpu.CompilerParams(vmem_limit_bytes=16 * 2**20),
    )(*outs)


def solution(mesh):
    return jax.shard_map(
        shards,
        mesh=mesh,
        in_specs=(
            P("fsdp", "blk", None),
            P("blk", None),
            P("blk", None),
            P("blk", None),
            P("blk", None),
            P("blk", None),
            P("blk", None),
        ),
        out_specs=(P("blk", None), P("blk", None), P("blk", None)),
        check_vma=False,
    )
```

```python
import functools

import jax
import jax.numpy as jnp
from jax import lax
from jax.experimental import pallas as pl
from jax.experimental.pallas import tpu as pltpu
from jax.sharding import PartitionSpec as P

BETA = 0.9
EPSILON = 1e-06
MESH = pl.DeviceIdType.MESH
F32 = jnp.float32
BF16 = jnp.bfloat16

ROWS = 256
ORDER = 1024
TEAM = 4
RING = 12
LANES = 128
CHUNK = 176
GROUP = 3 * CHUNK
PAIRS = 4

KEYS = (0, -3, 3, -1, 1, -4, 4, -2, 2, -5, 5, 6)
SLOT = {key: at for at, key in enumerate(KEYS)}
PIECES = ((0, 96), (96, 80))
DIAGONAL = (3, 5, 6)
LINKS = {1: (0, 1), 2: (1, 1), 4: (0, 4), 3: (4, -1), 5: (4, 1), 6: (4, 2)}


def tree(turn):
    links = {}
    for far, (near, step) in LINKS.items():
        if far == 6:
            links[6] = (-turn * near, turn * step)
        else:
            for s in (turn, -turn):
                links[-s * far] = (-s * near, s * step)
    return links


def depth(links, key):
    return 0 if key == 0 else 1 + depth(links, links[key][0])


def height(links, key):
    return max([1 + height(links, far) for far, (near, _) in links.items() if near == key], default=0)


def turn_of(piece):
    return 1 if piece % 2 == 0 else -1


def kernel(grads, l_codes, l_scales, r_codes, r_scales, l_stats, r_stats,
           update, l_out, r_out,
           x, acc, rbuf, gall, l_code_v, r_code_v, l_scale_v, r_scale_v,
           l_root, r_all, total, mixed, prod, sq,
           load_sem, rs_send, rs_recv, ag_send, ag_recv, y_send, y_recv, c_send, c_recv,
           r_send, r_recv, s_send, s_recv):
    z = lax.axis_index("fsdp")
    blk = lax.axis_index("blk")
    member = lax.rem(blk, TEAM)
    base = blk - member
    m_y = lax.rem(member + 2, TEAM)
    m_c = member + 1 - 2 * lax.rem(member, 2)
    m_yc = lax.rem(m_c + 2, TEAM)

    def ring(step, which=None):
        return (lax.rem(z + step + RING, RING), blk if which is None else base + which)

    def mate(which):
        return (z, base + which)

    barrier = pltpu.get_barrier_semaphore()
    steps = sorted({abs(step) for _, step in LINKS.values()})
    partners = [ring(s * step) for step in steps for s in (1, -1)] + [mate(m_y), mate(m_c), mate(m_yc)]
    cross = sorted({abs(LINKS[key][1]) for key in DIAGONAL})
    partners += [ring(s * step, m_y) for step in cross for s in (1, -1)]
    for partner in partners:
        pl.semaphore_signal(barrier, inc=1, device_id=partner, device_id_type=MESH)

    grad_loads = []
    for pair in range(PAIRS):
        for panel, row, rows, chunk, at in (
                (0, 0, 176, 0, 0), (0, 176, 80, 1, 0), (1, 0, 96, 1, 80), (1, 96, 160, 2, 0)):
            grad_loads.append(pltpu.make_async_copy(
                grads.at[0, pl.ds(row, rows), pl.ds((2 * pair + panel) * LANES, LANES)],
                x.at[3 * pair + chunk, pl.ds(at, rows)], load_sem.at[len(grad_loads)]))
    other = [
        pltpu.make_async_copy(r_scales, r_scale_v, load_sem.at[16]),
        pltpu.make_async_copy(r_codes, r_code_v, load_sem.at[17]),
        pltpu.make_async_copy(l_scales, l_scale_v, load_sem.at[18]),
        pltpu.make_async_copy(l_codes, l_code_v, load_sem.at[19]),
        pltpu.make_async_copy(l_stats, l_out, load_sem.at[20]),
        pltpu.make_async_copy(r_stats, r_out, load_sem.at[21]),
    ]
    for copy in grad_loads + other:
        copy.start()

    for pair in range(PAIRS):
        x[3 * pair + 2, pl.ds(160, 16), :] = jnp.zeros((16, LANES), BF16)
    pl.semaphore_wait(barrier, len(partners))

    def owner(key):
        return lax.rem(z + key + RING, RING)

    def remote(src, dst, send, recv, target):
        return pltpu.make_async_remote_copy(
            src_ref=src, dst_ref=dst, send_sem=send, recv_sem=recv,
            device_id=target, device_id_type=MESH)

    sends = []

    def rs_copy(src, key, piece):
        step = tree(turn_of(piece))[key][1]
        at = piece * 12 + SLOT[key]
        copy = remote(src, rbuf.at[SLOT[key], pl.ds(*PIECES[piece])], rs_send.at[at], rs_recv.at[at], ring(-step))
        copy.start()
        sends.append(copy)

    def rs_wait(key, piece):
        at = piece * 12 + SLOT[key]
        ref = rbuf.at[SLOT[key], pl.ds(*PIECES[piece])]
        remote(ref, ref, rs_send.at[at], rs_recv.at[at], ring(1)).wait_recv()
        return ref[...].astype(F32)

    def gathered(key, piece):
        links = tree(turn_of(piece))
        total = x[owner(key), pl.ds(*PIECES[piece]), :].astype(F32)
        beyond = [far for far in links if links[far][0] == key]
        for far in sorted(beyond, key=lambda far: height(links, far)):
            total = total + rs_wait(far, piece)
        return total.astype(BF16)

    for copy in grad_loads:
        copy.wait()
    for piece in range(len(PIECES)):
        links = tree(turn_of(piece))
        leaves = [key for key in links if height(links, key) == 0]
        for key in sorted(leaves, key=lambda key: (-depth(links, key), -abs(links[key][1]))):
            rs_copy(x.at[owner(key), pl.ds(*PIECES[piece])], key, piece)

    spread_group = lax.broadcasted_iota(jnp.int32, (48, ORDER), 0) % 16
    spread_column = lax.broadcasted_iota(jnp.int32, (48, ORDER), 1) // 64
    spread = jnp.where(spread_group == spread_column, 1.0, 0.0).astype(BF16)

    def dequantize(codes, scales):
        scaled = scales[...] * (1.0 / 15.0)
        first = scaled.astype(BF16)
        rest = scaled - first.astype(F32)
        second = rest.astype(BF16)
        third = (rest - second.astype(F32)).astype(BF16)
        terms = jnp.concatenate([first.astype(F32), second.astype(F32), third.astype(F32)], axis=0)
        wide = lax.dot_general(jnp.transpose(terms).astype(BF16), spread, (((1,), (0,)), ((), ())),
                               preferred_element_type=F32)
        return ((2.0 * codes[...].astype(F32) - 15.0) * wide).astype(BF16)

    for copy in other[:2]:
        copy.wait()
    r_all[member] = dequantize(r_code_v, r_scale_v)
    r_y = remote(r_all.at[member], r_all.at[member], r_send.at[0], r_recv.at[0], mate(m_y))
    r_c = remote(r_all.at[member], r_all.at[member], r_send.at[1], r_recv.at[1], mate(m_c))
    r_y.start()
    r_c.start()

    links = tree(1)
    for level in range(max(depth(links, key) for key in links), 0, -1):
        for piece in range(len(PIECES)):
            links = tree(turn_of(piece))
            nodes = [key for key in links if height(links, key) and depth(links, key) == level]
            for key in reversed(nodes):
                at = 6 * (level - 1) + nodes.index(key)
                cut = pl.ds(*PIECES[piece])
                acc[at, cut, :] = gathered(key, piece)
                rs_copy(acc.at[at, cut], key, piece)
        if level == 1:
            for copy in other[2:4]:
                copy.wait()
            left = dequantize(l_code_v, l_scale_v)
            for which in range(TEAM):
                l_root[which] = left[:, which * ROWS:(which + 1) * ROWS]

    def z_send(key, piece):
        links = tree(turn_of(piece))
        beyond = [far for far in links if links[far][0] == key]
        ref = gall.at[member, owner(key), pl.ds(*PIECES[piece])]
        for far in sorted(beyond, key=lambda far: (-height(links, far), abs(links[far][1]) * (1 if key else -1))):
            at = piece * 12 + SLOT[far]
            step = links[far][1]
            copies = [remote(ref, ref, ag_send.at[at], ag_recv.at[at], ring(step))]
            if abs(far) in DIAGONAL:
                copies.append(remote(ref, ref, y_send.at[at], y_recv.at[at], ring(step, m_y)))
            for copy in copies:
                copy.start()
                sends.append(copy)

    def z_wait(key, piece):
        at = piece * 12 + SLOT[key]
        ref = gall.at[member, owner(key), pl.ds(*PIECES[piece])]
        remote(ref, ref, ag_send.at[at], ag_recv.at[at], ring(1)).wait_recv()

    def y_forward(key, piece):
        if abs(key) in DIAGONAL:
            return
        at = piece * 12 + SLOT[key]
        ref = gall.at[member, owner(key), pl.ds(*PIECES[piece])]
        copy = remote(ref, ref, y_send.at[at], y_recv.at[at], mate(m_y))
        copy.start()
        sends.append(copy)

    def y_wait(key, piece):
        at = piece * 12 + SLOT[key]
        ref = gall.at[m_y, owner(key), pl.ds(*PIECES[piece])]
        remote(ref, ref, y_send.at[at], y_recv.at[at], mate(m_y)).wait_recv()

    def c_copy(which, piece, set_at):
        at = piece * 2 + set_at
        ref = gall.at[which, :, pl.ds(*PIECES[piece])]
        return remote(ref, ref, c_send.at[at], c_recv.at[at], mate(m_c))

    def c_forward(which, piece, set_at):
        copy = c_copy(which, piece, set_at)
        copy.start()
        sends.append(copy)

    for piece in range(len(PIECES)):
        gall[member, z, pl.ds(*PIECES[piece]), :] = gathered(0, piece)
        z_send(0, piece)
        y_forward(0, piece)
    links = tree(1)
    levels = max(depth(links, key) for key in links)
    for level in range(1, levels + 1):
        for piece in range(len(PIECES)):
            links = tree(turn_of(piece))
            for key in sorted([key for key in links if depth(links, key) == level],
                              key=lambda key: (-height(links, key), abs(links[key][1]))):
                z_wait(key, piece)
                z_send(key, piece)
                y_forward(key, piece)
            if level == levels:
                c_forward(member, piece, 0)
        if level == 1:
            remote(r_all.at[m_y], r_all.at[m_y], r_send.at[0], r_recv.at[0], mate(m_y)).wait_recv()
            r_yc = remote(r_all.at[m_y], r_all.at[m_y], r_send.at[2], r_recv.at[2], mate(m_c))
            r_yc.start()
    for piece in range(len(PIECES)):
        links = tree(turn_of(piece))
        for key in sorted(KEYS, key=lambda key: depth(links, key)):
            y_wait(key, piece)
        c_forward(m_y, piece, 1)
    def panel_pair(which, pair):
        both = gall[which, pl.ds(3 * pair, 3)].reshape(GROUP, LANES)
        return jnp.concatenate([both[:ROWS], both[ROWS:2 * ROWS]], axis=1)

    def rows_of(which):
        return jnp.concatenate([panel_pair(which, pair) for pair in range(PAIRS)], axis=1)

    def mix(which, first=False):
        part = jnp.dot(l_root[which], rows_of(which), preferred_element_type=F32)
        return part if first else total[...] + part

    scale = (1.0 - BETA) / ORDER

    def grams(which, first=False):
        cut = pl.ds(pl.multiple_of(which * ROWS, ROWS), ROWS)
        left = lax.dot_general(rows_of(member), rows_of(which), (((1,), (1,)), ((), ())), preferred_element_type=F32)
        l_out[:, cut] = BETA * l_out[:, cut] + scale * left
        right = jnp.dot(jnp.transpose(panel_pair(which, member)), rows_of(which), preferred_element_type=F32)
        r_out[...] = (BETA * r_out[...] if first else r_out[...]) + scale * right

    total[...] = mix(member, True)
    total[...] = mix(m_y)
    grad_square = jnp.sum(jnp.square(rows_of(member).astype(F32)), axis=0, keepdims=True)
    grad_square = sum(grad_square[:, at * LANES:(at + 1) * LANES] for at in range(8))
    for copy in other[4:]:
        copy.wait()
    grams(member, True)
    remote(r_all.at[m_c], r_all.at[m_c], r_send.at[1], r_recv.at[1], mate(m_c)).wait_recv()
    remote(r_all.at[m_yc], r_all.at[m_yc], r_send.at[2], r_recv.at[2], mate(m_c)).wait_recv()
    for piece in range(len(PIECES)):
        c_copy(m_c, piece, 0).wait_recv()
    total[...] = mix(m_c)
    for piece in range(len(PIECES)):
        c_copy(m_yc, piece, 1).wait_recv()
    mixed[...] = mix(m_yc).astype(BF16)
    square = jnp.zeros((ROWS, ROWS), F32)
    for pair in range(PAIRS):
        right = jnp.concatenate([r_all[which, :, pl.ds(pair * ROWS, ROWS)] for which in range(TEAM)], axis=0)
        part = jnp.dot(mixed[...], right, preferred_element_type=F32)
        prod[:, pl.ds(pair * ROWS, ROWS)] = part
        square = square + part * part
    prod_square = jnp.sum(square, axis=0, keepdims=True)
    prod_square = prod_square[:, :LANES] + prod_square[:, LANES:]
    sq[3] = jnp.concatenate(
        [jnp.broadcast_to(grad_square, (8, LANES)), jnp.broadcast_to(prod_square, (8, LANES))], axis=0)
    for at, which in enumerate((m_y, m_c, m_yc)):
        copy = remote(sq.at[3], sq.at[at], s_send.at[at], s_recv.at[at], mate(which))
        copy.start()
        sends.append(copy)
    for which in (m_y, m_c, m_yc):
        grams(which)

    for at in range(3):
        remote(sq.at[at], sq.at[at], s_send.at[at], s_recv.at[at], mate(m_y)).wait_recv()
    both = sq[0] + sq[1] + sq[2] + sq[3]
    entries = float(ORDER * ORDER)
    grad_mean = jnp.sum(both[0:1, :], axis=1, keepdims=True) / entries
    prod_mean = jnp.sum(both[8:9, :], axis=1, keepdims=True) / entries
    factor = jnp.sqrt(grad_mean) / jnp.sqrt(prod_mean + EPSILON)
    update[...] = (prod[...] * factor).astype(BF16)
    for copy in sends + [r_y, r_c, r_yc]:
        copy.wait_send()


def store_kernel(a, b, c, a_out, b_out, c_out, sem):
    copies = []
    for src, dst in ((b, b_out), (c, c_out), (a, a_out)):
        for part in range(4):
            cut = pl.ds(part * 64, 64)
            copies.append(pltpu.make_async_copy(src.at[cut], dst.at[cut], sem.at[len(copies)]))
    for copy in copies:
        copy.start()
    for copy in copies:
        copy.wait()


def shards(grads, l_codes, l_scales, r_codes, r_scales, l_stats, r_stats):
    any_spec = pl.BlockSpec(memory_space=pl.ANY)
    wide = (ROWS, ORDER)
    dma = pltpu.SemaphoreType.DMA
    pieces = len(PIECES)
    outs = pl.pallas_call(
        kernel,
        name="shampoo",
        out_shape=(
            pltpu.VMEM(wide, BF16),
            pltpu.VMEM(wide, F32),
            pltpu.VMEM(wide, F32),
        ),
        in_specs=[any_spec] * 7,
        out_specs=(pl.BlockSpec(memory_space=pltpu.VMEM),) * 3,
        scratch_shapes=[
            pltpu.VMEM((RING, CHUNK, LANES), BF16),
            pltpu.VMEM((36, CHUNK, LANES), BF16),
            pltpu.VMEM((12, CHUNK, LANES), BF16),
            pltpu.VMEM((TEAM, RING, CHUNK, LANES), BF16),
            pltpu.VMEM(wide, jnp.int32),
            pltpu.VMEM(wide, jnp.int32),
            pltpu.VMEM((16, ROWS), F32),
            pltpu.VMEM((16, ROWS), F32),
            pltpu.VMEM((TEAM, ROWS, ROWS), BF16),
            pltpu.VMEM((TEAM, ROWS, ORDER), BF16),
            pltpu.VMEM(wide, F32),
            pltpu.VMEM(wide, BF16),
            pltpu.VMEM(wide, F32),
            pltpu.VMEM((4, 16, LANES), F32),
            dma((22,)), dma((12 * pieces,)), dma((12 * pieces,)), dma((12 * pieces,)), dma((12 * pieces,)),
            dma((12 * pieces,)), dma((12 * pieces,)), dma((2 * pieces,)), dma((2 * pieces,)),
            dma((3,)), dma((3,)), dma((3,)), dma((3,)),
        ],
        compiler_params=pltpu.CompilerParams(
            collective_id=0, has_side_effects=True, vmem_limit_bytes=40 * 2**20),
    )(*[pltpu.with_memory_space_constraint(a, pltpu.HBM) for a in (grads, l_codes, l_scales.T, r_codes, r_scales.T, l_stats, r_stats)])
    return pl.pallas_call(
        store_kernel,
        name="store",
        out_shape=(pltpu.HBM(wide, BF16), pltpu.HBM(wide, F32), pltpu.HBM(wide, F32)),
        in_specs=[any_spec] * 3,
        out_specs=(any_spec,) * 3,
        scratch_shapes=[dma((12,))],
        compiler_params=pltpu.CompilerParams(vmem_limit_bytes=16 * 2**20),
    )(*outs)


def solution(mesh):
    return jax.shard_map(
        shards,
        mesh=mesh,
        in_specs=(
            P("fsdp", "blk", None),
            P("blk", None),
            P("blk", None),
            P("blk", None),
            P("blk", None),
            P("blk", None),
            P("blk", None),
        ),
        out_specs=(P("blk", None), P("blk", None), P("blk", None)),
        check_vma=False,
    )
```

```python
import functools

import jax
import jax.numpy as jnp
from jax import lax
from jax.experimental import pallas as pl
from jax.experimental.pallas import tpu as pltpu
from jax.sharding import PartitionSpec as P

BETA = 0.9
EPSILON = 1e-06
MESH = pl.DeviceIdType.MESH
F32 = jnp.float32
BF16 = jnp.bfloat16

ROWS = 256
ORDER = 1024
TEAM = 4
RING = 12
LANES = 128
CHUNK = 176
GROUP = 3 * CHUNK
PAIRS = 4

KEYS = (0, -3, -5, 6, 5, 3, -1, 1, -4, 4, -2, 2)
SLOT = {key: at for at, key in enumerate(KEYS[1:])}
SUM_WAIT = {-4: 0, 4: 1, 0: 2, -1: 3, 1: 4}
SPREAD_WAIT = {-1: 0, 1: 1, -4: 2, 4: 3, -2: 4, 2: 5, -3: 6, 3: 6, -5: 6, 5: 6, 6: 6}
PIECES = ((0, 80), (80, 96))
DIAGONAL = (3, 5, 6)
LINKS = {1: (0, 1), 2: (1, 1), 4: (0, 4), 3: (4, -1), 5: (4, 1), 6: (4, 2)}


def tree(turn):
    links = {}
    for far, (near, step) in LINKS.items():
        if far == 6:
            links[6] = (-turn * near, turn * step)
        else:
            for s in (turn, -turn):
                links[-s * far] = (-s * near, s * step)
    return links


def depth(links, key):
    return 0 if key == 0 else 1 + depth(links, links[key][0])


def height(links, key):
    return max([1 + height(links, far) for far, (near, _) in links.items() if near == key], default=0)


def turn_of(piece):
    return 1 if piece % 2 == 0 else -1


def kernel(grads, l_codes, l_scales, r_codes, r_scales, l_stats, r_stats,
           prod, l_out, r_out, factor,
           x, acc, rbuf, gall, l_code_v, r_code_v, l_scale_v, r_scale_v,
           l_root, r_all, total, mixed, sq,
           load_sem, rs_send, rs_recv, ag_send, ag_recv, y_send, y_recv, c_send, c_recv,
           r_send, r_recv, s_send, s_recv):
    z = lax.axis_index("fsdp")
    blk = lax.axis_index("blk")
    member = lax.rem(blk, TEAM)
    base = blk - member
    m_y = lax.rem(member + 2, TEAM)
    m_c = member + 1 - 2 * lax.rem(member, 2)
    m_yc = lax.rem(m_c + 2, TEAM)

    def ring(step, which=None):
        return (lax.rem(z + step + RING, RING), blk if which is None else base + which)

    def mate(which):
        return (z, base + which)

    barrier = pltpu.get_barrier_semaphore()
    steps = sorted({abs(step) for _, step in LINKS.values()})
    partners = [ring(s * step) for step in reversed(steps) for s in (1, -1)] + [mate(m_y), mate(m_c), mate(m_yc)]
    cross = sorted({abs(LINKS[key][1]) for key in DIAGONAL})
    partners += [ring(s * step, m_y) for step in cross for s in (1, -1)]
    for partner in partners:
        pl.semaphore_signal(barrier, inc=1, device_id=partner, device_id_type=MESH)

    grad_loads = []
    for pair in range(PAIRS):
        for panel, row, rows, chunk, at in (
                (0, 0, 176, 0, 0), (0, 176, 80, 1, 0), (1, 0, 96, 1, 80), (1, 96, 160, 2, 0)):
            grad_loads.append(pltpu.make_async_copy(
                grads.at[0, pl.ds(row, rows), pl.ds((2 * pair + panel) * LANES, LANES)],
                x.at[3 * pair + chunk, pl.ds(at, rows)], load_sem.at[len(grad_loads)]))
    other = [
        pltpu.make_async_copy(r_scales, r_scale_v, load_sem.at[16]),
        pltpu.make_async_copy(r_codes, r_code_v, load_sem.at[17]),
        pltpu.make_async_copy(l_scales, l_scale_v, load_sem.at[18]),
        pltpu.make_async_copy(l_codes, l_code_v, load_sem.at[19]),
        pltpu.make_async_copy(l_stats, l_out, load_sem.at[20]),
        pltpu.make_async_copy(r_stats, r_out, load_sem.at[21]),
    ]
    for copy in grad_loads + other:
        copy.start()

    for pair in range(PAIRS):
        x[3 * pair + 2, pl.ds(160, 16), :] = jnp.zeros((16, LANES), BF16)
    pl.semaphore_wait(barrier, len(partners))

    def owner(key):
        return lax.rem(z + key + RING, RING)

    def remote(src, dst, send, recv, target):
        return pltpu.make_async_remote_copy(
            src_ref=src, dst_ref=dst, send_sem=send, recv_sem=recv,
            device_id=target, device_id_type=MESH)

    sends = []

    def rs_copy(src, key, piece):
        near, step = tree(turn_of(piece))[key]
        ref = rbuf.at[SLOT[key], pl.ds(*PIECES[piece])]
        remote(src, ref, rs_send.at[piece], rs_recv.at[5 * piece + SUM_WAIT[near]], ring(-step)).start()

    def gathered(key, piece):
        links = tree(turn_of(piece))
        cut = pl.ds(*PIECES[piece])
        slots = sorted(SLOT[far] for far in links if links[far][0] == key)
        ref = rbuf.at[pl.ds(slots[0], len(slots)), cut]
        remote(ref, ref, rs_send.at[piece], rs_recv.at[5 * piece + SUM_WAIT[key]], ring(1)).wait_recv()
        result = x[owner(key), cut, :].astype(F32)
        for slot in slots:
            result = result + rbuf[slot, cut, :].astype(F32)
        return result.astype(BF16)

    for copy in grad_loads:
        copy.wait()
    for piece in range(len(PIECES)):
        links = tree(turn_of(piece))
        leaves = [key for key in links if height(links, key) == 0]
        for key in sorted(leaves, key=lambda key: (-depth(links, key), -abs(links[key][1]))):
            rs_copy(x.at[owner(key), pl.ds(*PIECES[piece])], key, piece)

    spread_group = lax.broadcasted_iota(jnp.int32, (48, ORDER), 0) % 16
    spread_column = lax.broadcasted_iota(jnp.int32, (48, ORDER), 1) // 64
    spread = jnp.where(spread_group == spread_column, 1.0, 0.0).astype(BF16)

    def dequantize(codes, scales):
        scaled = scales[...] * (1.0 / 15.0)
        first = scaled.astype(BF16)
        rest = scaled - first.astype(F32)
        second = rest.astype(BF16)
        third = (rest - second.astype(F32)).astype(BF16)
        terms = jnp.concatenate([first.astype(F32), second.astype(F32), third.astype(F32)], axis=0)
        wide = lax.dot_general(jnp.transpose(terms).astype(BF16), spread, (((1,), (0,)), ((), ())),
                               preferred_element_type=F32)
        return ((2.0 * codes[...].astype(F32) - 15.0) * wide).astype(BF16)

    for copy in other[:2]:
        copy.wait()
    r_all[member] = dequantize(r_code_v, r_scale_v)
    r_y = remote(r_all.at[member], r_all.at[member], r_send.at[0], r_recv.at[0], mate(m_y))
    r_c = remote(r_all.at[member], r_all.at[member], r_send.at[1], r_recv.at[1], mate(m_c))
    r_y.start()
    r_c.start()

    links = tree(1)
    for level in range(max(depth(links, key) for key in links), 0, -1):
        for piece in range(len(PIECES)):
            links = tree(turn_of(piece))
            nodes = [key for key in links if height(links, key) and depth(links, key) == level]
            for key in reversed(nodes):
                at = 6 * (level - 1) + nodes.index(key)
                cut = pl.ds(*PIECES[piece])
                acc[at, cut, :] = gathered(key, piece)
                rs_copy(acc.at[at, cut], key, piece)
        if level == 1:
            for copy in other[2:4]:
                copy.wait()
            left = dequantize(l_code_v, l_scale_v)
            for which in range(TEAM):
                l_root[which] = left[:, which * ROWS:(which + 1) * ROWS]

    def z_send(key, piece):
        links = tree(turn_of(piece))
        beyond = [far for far in links if links[far][0] == key]
        ref = gall.at[member, owner(key), pl.ds(*PIECES[piece])]
        for far in sorted(beyond, key=lambda far: (-height(links, far), abs(links[far][1]) * (1 if key else -1))):
            at = 7 * piece + SPREAD_WAIT[far]
            step = links[far][1]
            remote(ref, ref, ag_send.at[piece], ag_recv.at[at], ring(step)).start()
            if abs(far) in DIAGONAL:
                remote(ref, ref, y_send.at[piece], y_recv.at[piece], ring(step, m_y)).start()

    def z_wait(key, piece):
        at = 7 * piece + SPREAD_WAIT[key]
        count = sum(1 for other_key in SPREAD_WAIT if SPREAD_WAIT[other_key] == SPREAD_WAIT[key])
        ref = gall.at[member, pl.ds(0, count), pl.ds(*PIECES[piece])]
        remote(ref, ref, ag_send.at[piece], ag_recv.at[at], ring(1)).wait_recv()

    def y_forward(key, piece):
        ref = gall.at[member, owner(key), pl.ds(*PIECES[piece])]
        remote(ref, ref, y_send.at[piece], y_recv.at[piece], mate(m_y)).start()

    def y_wait(piece):
        ref = gall.at[m_y, :, pl.ds(*PIECES[piece])]
        remote(ref, ref, y_send.at[piece], y_recv.at[piece], mate(m_y)).wait_recv()

    def c_copy(which, piece, set_at):
        at = piece * 2 + set_at
        ref = gall.at[which, :, pl.ds(*PIECES[piece])]
        return remote(ref, ref, c_send.at[at], c_recv.at[at], mate(m_c))

    def c_forward(which, piece, set_at):
        copy = c_copy(which, piece, set_at)
        copy.start()
        sends.append(copy)

    for piece in range(len(PIECES)):
        gall[member, z, pl.ds(*PIECES[piece]), :] = gathered(0, piece)
        z_send(0, piece)
        y_forward(0, piece)
    links = tree(1)
    levels = max(depth(links, key) for key in links)
    for level in range(1, levels + 1):
        for piece in range(len(PIECES)):
            links = tree(turn_of(piece))
            here = [key for key in links if depth(links, key) == level and abs(key) not in DIAGONAL]
            for key in sorted(here, key=lambda key: (-height(links, key), abs(links[key][1]))):
                z_wait(key, piece)
                z_send(key, piece)
                y_forward(key, piece)
            if level == levels:
                z_wait(6, piece)
                c_forward(member, piece, 0)
        if level == 1:
            remote(r_all.at[m_y], r_all.at[m_y], r_send.at[0], r_recv.at[0], mate(m_y)).wait_recv()
            r_yc = remote(r_all.at[m_y], r_all.at[m_y], r_send.at[2], r_recv.at[2], mate(m_c))
            r_yc.start()
    for piece in range(len(PIECES)):
        y_wait(piece)
        c_forward(m_y, piece, 1)

    def panel_pair(which, pair):
        both = gall[which, pl.ds(3 * pair, 3)].reshape(GROUP, LANES)
        return jnp.concatenate([both[:ROWS], both[ROWS:2 * ROWS]], axis=1)

    def rows_of(which):
        return jnp.concatenate([panel_pair(which, pair) for pair in range(PAIRS)], axis=1)

    def mix(which, first=False):
        part = jnp.dot(l_root[which], rows_of(which), preferred_element_type=F32)
        return part if first else total[...] + part

    scale = (1.0 - BETA) / ORDER

    def grams(which, first=False):
        cut = pl.ds(pl.multiple_of(which * ROWS, ROWS), ROWS)
        left = lax.dot_general(rows_of(member), rows_of(which), (((1,), (1,)), ((), ())), preferred_element_type=F32)
        l_out[:, cut] = BETA * l_out[:, cut] + scale * left
        right = jnp.dot(jnp.transpose(panel_pair(which, member)), rows_of(which), preferred_element_type=F32)
        r_out[...] = (BETA * r_out[...] if first else r_out[...]) + scale * right

    total[...] = mix(member, True)
    total[...] = mix(m_y)
    grad_square = jnp.sum(jnp.square(rows_of(member).astype(F32)), axis=0, keepdims=True)
    grad_square = sum(grad_square[:, at * LANES:(at + 1) * LANES] for at in range(8))
    for copy in other[4:]:
        copy.wait()
    grams(member, True)
    remote(r_all.at[m_c], r_all.at[m_c], r_send.at[1], r_recv.at[1], mate(m_c)).wait_recv()
    remote(r_all.at[m_yc], r_all.at[m_yc], r_send.at[2], r_recv.at[2], mate(m_c)).wait_recv()
    for piece in range(len(PIECES)):
        c_copy(m_c, piece, 0).wait_recv()
    total[...] = mix(m_c)
    for piece in range(len(PIECES)):
        c_copy(m_yc, piece, 1).wait_recv()
    mixed[...] = mix(m_yc).astype(BF16)
    square = jnp.zeros((ROWS, ROWS), F32)
    for pair in range(PAIRS):
        right = jnp.concatenate([r_all[which, :, pl.ds(pair * ROWS, ROWS)] for which in range(TEAM)], axis=0)
        part = jnp.dot(mixed[...], right, preferred_element_type=F32)
        prod[:, pl.ds(pair * ROWS, ROWS)] = part
        square = square + part * part
    prod_square = jnp.sum(square, axis=0, keepdims=True)
    prod_square = prod_square[:, :LANES] + prod_square[:, LANES:]
    sq[3] = jnp.concatenate(
        [jnp.broadcast_to(grad_square, (8, LANES)), jnp.broadcast_to(prod_square, (8, LANES))], axis=0)
    for at, which in enumerate((m_y, m_c, m_yc)):
        copy = remote(sq.at[3], sq.at[at], s_send.at[at], s_recv.at[at], mate(which))
        copy.start()
        sends.append(copy)
    for which in (m_y, m_c, m_yc):
        grams(which)

    for copy in sends[:-3] + [r_y, r_c, r_yc]:
        copy.wait_send()
    for piece in range(len(PIECES)):
        cut = pl.ds(*PIECES[piece])
        ref = rbuf.at[:, cut]
        remote(ref, ref, rs_send.at[piece], rs_recv.at[5 * piece], ring(1)).wait_send()
        ref = gall.at[member, pl.ds(0, 11), cut]
        remote(ref, ref, ag_send.at[piece], ag_recv.at[7 * piece], ring(1)).wait_send()
        ref = gall.at[member, :, cut]
        remote(ref, ref, y_send.at[piece], y_recv.at[piece], mate(m_y)).wait_send()
    for at in range(3):
        remote(sq.at[at], sq.at[at], s_send.at[at], s_recv.at[at], mate(m_y)).wait_recv()
    both = sq[0] + sq[1] + sq[2] + sq[3]
    entries = float(ORDER * ORDER)
    grad_mean = jnp.sum(both[0:8, :], axis=1, keepdims=True) / entries
    prod_mean = jnp.sum(both[8:16, :], axis=1, keepdims=True) / entries
    factor[...] = jnp.broadcast_to(jnp.sqrt(grad_mean) / jnp.sqrt(prod_mean + EPSILON), (8, LANES))
    for copy in sends[-3:]:
        copy.wait_send()


def store_kernel(prod, l_new, r_new, factor, update, l_out, r_out, scaled, sem):
    copies = [
        pltpu.make_async_copy(l_new, l_out, sem.at[0]),
        pltpu.make_async_copy(r_new, r_out, sem.at[1]),
        pltpu.make_async_copy(scaled, update, sem.at[2]),
    ]
    for copy in copies[:2]:
        copy.start()
    scaled[...] = (prod[...] * factor[0:1, 0:1]).astype(BF16)
    copies[2].start()
    for copy in copies:
        copy.wait()


def shards(grads, l_codes, l_scales, r_codes, r_scales, l_stats, r_stats):
    any_spec = pl.BlockSpec(memory_space=pl.ANY)
    vmem_spec = pl.BlockSpec(memory_space=pltpu.VMEM)
    wide = (ROWS, ORDER)
    dma = pltpu.SemaphoreType.DMA
    pieces = len(PIECES)
    outs = pl.pallas_call(
        kernel,
        name="shampoo",
        out_shape=(
            pltpu.VMEM(wide, F32),
            pltpu.VMEM(wide, F32),
            pltpu.VMEM(wide, F32),
            pltpu.VMEM((8, LANES), F32),
        ),
        in_specs=[any_spec] * 7,
        out_specs=(vmem_spec,) * 4,
        scratch_shapes=[
            pltpu.VMEM((RING, CHUNK, LANES), BF16),
            pltpu.VMEM((36, CHUNK, LANES), BF16),
            pltpu.VMEM((11, CHUNK, LANES), BF16),
            pltpu.VMEM((TEAM, RING, CHUNK, LANES), BF16),
            pltpu.VMEM(wide, jnp.int32),
            pltpu.VMEM(wide, jnp.int32),
            pltpu.VMEM((16, ROWS), F32),
            pltpu.VMEM((16, ROWS), F32),
            pltpu.VMEM((TEAM, ROWS, ROWS), BF16),
            pltpu.VMEM((TEAM, ROWS, ORDER), BF16),
            pltpu.VMEM(wide, F32),
            pltpu.VMEM(wide, BF16),
            pltpu.VMEM((4, 16, LANES), F32),
            dma((22,)), dma((pieces,)), dma((5 * pieces,)), dma((pieces,)), dma((7 * pieces,)),
            dma((pieces,)), dma((pieces,)), dma((2 * pieces,)), dma((2 * pieces,)),
            dma((3,)), dma((3,)), dma((3,)), dma((3,)),
        ],
        compiler_params=pltpu.CompilerParams(
            collective_id=0, has_side_effects=True, vmem_limit_bytes=40 * 2**20),
    )(*[pltpu.with_memory_space_constraint(a, pltpu.HBM) for a in (grads, l_codes, l_scales.T, r_codes, r_scales.T, l_stats, r_stats)])
    return pl.pallas_call(
        store_kernel,
        name="store",
        out_shape=(pltpu.HBM(wide, BF16), pltpu.HBM(wide, F32), pltpu.HBM(wide, F32)),
        in_specs=[vmem_spec] * 4,
        out_specs=(any_spec,) * 3,
        scratch_shapes=[pltpu.VMEM(wide, BF16), dma((3,))],
        compiler_params=pltpu.CompilerParams(vmem_limit_bytes=16 * 2**20),
    )(*outs)


def solution(mesh):
    return jax.shard_map(
        shards,
        mesh=mesh,
        in_specs=(
            P("fsdp", "blk", None),
            P("blk", None),
            P("blk", None),
            P("blk", None),
            P("blk", None),
            P("blk", None),
            P("blk", None),
        ),
        out_specs=(P("blk", None), P("blk", None), P("blk", None)),
        check_vma=False,
    )
```

```python
import functools

import jax
import jax.numpy as jnp
from jax import lax
from jax.experimental import pallas as pl
from jax.experimental.pallas import tpu as pltpu
from jax.sharding import PartitionSpec as P

BETA = 0.9
EPSILON = 1e-06
MESH = pl.DeviceIdType.MESH
F32 = jnp.float32
BF16 = jnp.bfloat16

ROWS = 256
ORDER = 1024
TEAM = 4
RING = 12
LANES = 128
CHUNK = 176
GROUP = 3 * CHUNK
PAIRS = 4

KEYS = (0, -3, -5, 6, 5, 3, -1, 1, -4, 4, -2, 2)
SLOT = {key: at for at, key in enumerate(KEYS[1:])}
SUM_WAIT = {-4: 0, 4: 1, 0: 2, -1: 3, 1: 4}
SPREAD_WAIT = {-1: 0, 1: 1, -4: 2, 4: 3, -2: 4, 2: 4, -3: 4, 3: 4, -5: 4, 5: 4, 6: 4}
PIECES = ((0, 80), (80, 96))
DIAGONAL = (2, 3, 5, 6)
LINKS = {1: (0, 1), 2: (1, 1), 4: (0, 4), 3: (4, -1), 5: (4, 1), 6: (4, 2)}


def tree(turn):
    links = {}
    for far, (near, step) in LINKS.items():
        if far == 6:
            links[6] = (-turn * near, turn * step)
        else:
            for s in (turn, -turn):
                links[-s * far] = (-s * near, s * step)
    return links


def depth(links, key):
    return 0 if key == 0 else 1 + depth(links, links[key][0])


def height(links, key):
    return max([1 + height(links, far) for far, (near, _) in links.items() if near == key], default=0)


def turn_of(piece):
    return 1 if piece % 2 == 0 else -1


def kernel(grads, l_codes, l_scales, r_codes, r_scales, l_stats, r_stats,
           prod, l_out, r_out, factor,
           x, acc, rbuf, gall, l_code_v, r_code_v, l_scale_v, r_scale_v,
           l_root, r_all, total, mixed, sq,
           load_sem, rs_send, rs_recv, ag_send, ag_recv, y_send, y_recv, c_send, c_recv,
           r_send, r_recv, s_send, s_recv):
    z = lax.axis_index("fsdp")
    blk = lax.axis_index("blk")
    member = lax.rem(blk, TEAM)
    base = blk - member
    m_y = lax.rem(member + 2, TEAM)
    m_c = member + 1 - 2 * lax.rem(member, 2)
    m_yc = lax.rem(m_c + 2, TEAM)

    def ring(step, which=None):
        return (lax.rem(z + step + RING, RING), blk if which is None else base + which)

    def mate(which):
        return (z, base + which)

    barrier = pltpu.get_barrier_semaphore()
    steps = sorted({abs(step) for _, step in LINKS.values()})
    partners = [ring(s * step) for step in reversed(steps) for s in (1, -1)] + [mate(m_y), mate(m_c), mate(m_yc)]
    cross = sorted({abs(LINKS[key][1]) for key in DIAGONAL})
    partners += [ring(s * step, m_y) for step in cross for s in (1, -1)]
    for partner in partners:
        pl.semaphore_signal(barrier, inc=1, device_id=partner, device_id_type=MESH)

    grad_loads = []
    for pair in range(PAIRS):
        for panel, row, rows, chunk, at in (
                (0, 0, 176, 0, 0), (0, 176, 80, 1, 0), (1, 0, 96, 1, 80), (1, 96, 160, 2, 0)):
            grad_loads.append(pltpu.make_async_copy(
                grads.at[0, pl.ds(row, rows), pl.ds((2 * pair + panel) * LANES, LANES)],
                x.at[3 * pair + chunk, pl.ds(at, rows)], load_sem.at[6]))
    other = [
        pltpu.make_async_copy(r_scales, r_scale_v, load_sem.at[0]),
        pltpu.make_async_copy(r_codes, r_code_v, load_sem.at[1]),
        pltpu.make_async_copy(l_scales, l_scale_v, load_sem.at[2]),
        pltpu.make_async_copy(l_codes, l_code_v, load_sem.at[3]),
        pltpu.make_async_copy(l_stats, l_out, load_sem.at[4]),
        pltpu.make_async_copy(r_stats, r_out, load_sem.at[5]),
    ]
    for copy in grad_loads + other:
        copy.start()

    for pair in range(PAIRS):
        x[3 * pair + 2, pl.ds(160, 16), :] = jnp.zeros((16, LANES), BF16)
    pl.semaphore_wait(barrier, len(partners))

    def owner(key):
        return lax.rem(z + key + RING, RING)

    def remote(src, dst, send, recv, target):
        return pltpu.make_async_remote_copy(
            src_ref=src, dst_ref=dst, send_sem=send, recv_sem=recv,
            device_id=target, device_id_type=MESH)

    sends = []

    def rs_copy(src, key, piece):
        near, step = tree(turn_of(piece))[key]
        ref = rbuf.at[SLOT[key], pl.ds(*PIECES[piece])]
        remote(src, ref, rs_send.at[piece], rs_recv.at[5 * piece + SUM_WAIT[near]], ring(-step)).start()

    def gathered(key, piece):
        links = tree(turn_of(piece))
        cut = pl.ds(*PIECES[piece])
        slots = sorted(SLOT[far] for far in links if links[far][0] == key)
        ref = rbuf.at[pl.ds(slots[0], len(slots)), cut]
        remote(ref, ref, rs_send.at[piece], rs_recv.at[5 * piece + SUM_WAIT[key]], ring(1)).wait_recv()
        result = x[owner(key), cut, :].astype(F32)
        for slot in slots:
            result = result + rbuf[slot, cut, :].astype(F32)
        return result.astype(BF16)

    pltpu.make_async_copy(grads.at[0], mixed, load_sem.at[6]).wait()
    for piece in range(len(PIECES)):
        links = tree(turn_of(piece))
        leaves = [key for key in links if height(links, key) == 0]
        for key in sorted(leaves, key=lambda key: (-depth(links, key), -abs(links[key][1]))):
            rs_copy(x.at[owner(key), pl.ds(*PIECES[piece])], key, piece)

    spread_group = lax.broadcasted_iota(jnp.int32, (48, ORDER), 0) % 16
    spread_column = lax.broadcasted_iota(jnp.int32, (48, ORDER), 1) // 64
    spread = jnp.where(spread_group == spread_column, 1.0, 0.0).astype(BF16)

    def dequantize(codes, scales):
        scaled = scales[...] * (1.0 / 15.0)
        first = scaled.astype(BF16)
        rest = scaled - first.astype(F32)
        second = rest.astype(BF16)
        third = (rest - second.astype(F32)).astype(BF16)
        terms = jnp.concatenate([first.astype(F32), second.astype(F32), third.astype(F32)], axis=0)
        wide = lax.dot_general(jnp.transpose(terms).astype(BF16), spread, (((1,), (0,)), ((), ())),
                               preferred_element_type=F32)
        return ((2.0 * codes[...].astype(F32) - 15.0) * wide).astype(BF16)

    for copy in other[:2]:
        copy.wait()
    r_all[member] = dequantize(r_code_v, r_scale_v)
    r_y = remote(r_all.at[member], r_all.at[member], r_send.at[0], r_recv.at[0], mate(m_y))
    r_c = remote(r_all.at[member], r_all.at[member], r_send.at[1], r_recv.at[1], mate(m_c))
    r_y.start()
    r_c.start()

    links = tree(1)
    for level in range(max(depth(links, key) for key in links), 0, -1):
        for piece in range(len(PIECES)):
            links = tree(turn_of(piece))
            nodes = [key for key in links if height(links, key) and depth(links, key) == level]
            for key in reversed(nodes):
                at = 6 * (level - 1) + nodes.index(key)
                cut = pl.ds(*PIECES[piece])
                acc[at, cut, :] = gathered(key, piece)
                rs_copy(acc.at[at, cut], key, piece)
        if level == 1:
            for copy in other[2:4]:
                copy.wait()
            left = dequantize(l_code_v, l_scale_v)
            for which in range(TEAM):
                l_root[which] = left[:, which * ROWS:(which + 1) * ROWS]

    def z_send(key, piece):
        links = tree(turn_of(piece))
        beyond = [far for far in links if links[far][0] == key]
        ref = gall.at[member, owner(key), pl.ds(*PIECES[piece])]
        for far in sorted(beyond, key=lambda far: (-height(links, far), abs(links[far][1]) * (1 if key else -1))):
            at = 5 * piece + SPREAD_WAIT[far]
            step = links[far][1]
            remote(ref, ref, ag_send.at[piece], ag_recv.at[at], ring(step)).start()
            if abs(far) in DIAGONAL:
                remote(ref, ref, y_send.at[piece], y_recv.at[piece], ring(step, m_y)).start()

    def z_wait(key, piece):
        at = 5 * piece + SPREAD_WAIT[key]
        count = sum(1 for other_key in SPREAD_WAIT if SPREAD_WAIT[other_key] == SPREAD_WAIT[key])
        ref = gall.at[member, pl.ds(0, count), pl.ds(*PIECES[piece])]
        remote(ref, ref, ag_send.at[piece], ag_recv.at[at], ring(1)).wait_recv()

    def y_forward(key, piece):
        ref = gall.at[member, owner(key), pl.ds(*PIECES[piece])]
        remote(ref, ref, y_send.at[piece], y_recv.at[piece], mate(m_y)).start()

    def y_wait(piece):
        ref = gall.at[m_y, :, pl.ds(*PIECES[piece])]
        remote(ref, ref, y_send.at[piece], y_recv.at[piece], mate(m_y)).wait_recv()

    def c_copy(which, piece, set_at):
        at = piece * 2 + set_at
        ref = gall.at[which, :, pl.ds(*PIECES[piece])]
        return remote(ref, ref, c_send.at[at], c_recv.at[at], mate(m_c))

    def c_forward(which, piece, set_at):
        copy = c_copy(which, piece, set_at)
        copy.start()
        sends.append(copy)

    for piece in range(len(PIECES)):
        gall[member, z, pl.ds(*PIECES[piece]), :] = gathered(0, piece)
        z_send(0, piece)
        y_forward(0, piece)
    links = tree(1)
    levels = max(depth(links, key) for key in links)
    for level in range(1, levels + 1):
        for piece in range(len(PIECES)):
            links = tree(turn_of(piece))
            here = [key for key in links if depth(links, key) == level and abs(key) not in DIAGONAL]
            for key in sorted(here, key=lambda key: (-height(links, key), abs(links[key][1]))):
                z_wait(key, piece)
                z_send(key, piece)
                y_forward(key, piece)
            if level == levels:
                z_wait(6, piece)
                c_forward(member, piece, 0)
        if level == 1:
            remote(r_all.at[m_y], r_all.at[m_y], r_send.at[0], r_recv.at[0], mate(m_y)).wait_recv()
            r_yc = remote(r_all.at[m_y], r_all.at[m_y], r_send.at[2], r_recv.at[2], mate(m_c))
            r_yc.start()
    for piece in range(len(PIECES)):
        y_wait(piece)
        c_forward(m_y, piece, 1)

    def panel_pair(which, pair):
        both = gall[which, pl.ds(3 * pair, 3)].reshape(GROUP, LANES)
        return jnp.concatenate([both[:ROWS], both[ROWS:2 * ROWS]], axis=1)

    def rows_of(which):
        return jnp.concatenate([panel_pair(which, pair) for pair in range(PAIRS)], axis=1)

    def mix(which, first=False):
        part = jnp.dot(l_root[which], rows_of(which), preferred_element_type=F32)
        return part if first else total[...] + part

    scale = (1.0 - BETA) / ORDER

    def grams(which, first=False):
        cut = pl.ds(pl.multiple_of(which * ROWS, ROWS), ROWS)
        left = lax.dot_general(rows_of(member), rows_of(which), (((1,), (1,)), ((), ())), preferred_element_type=F32)
        l_out[:, cut] = BETA * l_out[:, cut] + scale * left
        right = jnp.dot(jnp.transpose(panel_pair(which, member)), rows_of(which), preferred_element_type=F32)
        r_out[...] = (BETA * r_out[...] if first else r_out[...]) + scale * right

    total[...] = mix(member, True)
    total[...] = mix(m_y)
    grad_square = jnp.sum(jnp.square(rows_of(member).astype(F32)), axis=0, keepdims=True)
    grad_square = sum(grad_square[:, at * LANES:(at + 1) * LANES] for at in range(8))
    remote(r_all.at[m_c], r_all.at[m_c], r_send.at[1], r_recv.at[1], mate(m_c)).wait_recv()
    remote(r_all.at[m_yc], r_all.at[m_yc], r_send.at[2], r_recv.at[2], mate(m_c)).wait_recv()
    for piece in range(len(PIECES)):
        c_copy(m_c, piece, 0).wait_recv()
    total[...] = mix(m_c)
    for piece in range(len(PIECES)):
        c_copy(m_yc, piece, 1).wait_recv()
    mixed[...] = mix(m_yc).astype(BF16)
    square = jnp.zeros((ROWS, ROWS), F32)
    for pair in range(PAIRS):
        right = jnp.concatenate([r_all[which, :, pl.ds(pair * ROWS, ROWS)] for which in range(TEAM)], axis=0)
        part = jnp.dot(mixed[...], right, preferred_element_type=F32)
        prod[:, pl.ds(pair * ROWS, ROWS)] = part
        square = square + part * part
    prod_square = jnp.sum(square, axis=0, keepdims=True)
    prod_square = prod_square[:, :LANES] + prod_square[:, LANES:]
    sq[3] = jnp.concatenate(
        [jnp.broadcast_to(grad_square, (8, LANES)), jnp.broadcast_to(prod_square, (8, LANES))], axis=0)
    for at, which in enumerate((m_y, m_c, m_yc)):
        remote(sq.at[3], sq.at[at], s_send.at[0], s_recv.at[0], mate(which)).start()
    for copy in other[4:]:
        copy.wait()
    grams(member, True)
    for which in (m_y, m_c, m_yc):
        grams(which)

    for copy in sends + [r_y, r_c, r_yc]:
        copy.wait_send()
    for piece in range(len(PIECES)):
        cut = pl.ds(*PIECES[piece])
        ref = rbuf.at[:, cut]
        remote(ref, ref, rs_send.at[piece], rs_recv.at[5 * piece], ring(1)).wait_send()
        ref = gall.at[member, pl.ds(0, 11), cut]
        remote(ref, ref, ag_send.at[piece], ag_recv.at[5 * piece], ring(1)).wait_send()
        ref = gall.at[member, :, cut]
        remote(ref, ref, y_send.at[piece], y_recv.at[piece], mate(m_y)).wait_send()
    squares = remote(sq.at[pl.ds(0, 3)], sq.at[pl.ds(0, 3)], s_send.at[0], s_recv.at[0], mate(m_y))
    squares.wait_recv()
    both = sq[0] + sq[1] + sq[2] + sq[3]
    entries = float(ORDER * ORDER)
    grad_mean = jnp.sum(both[0:8, :], axis=1, keepdims=True) / entries
    prod_mean = jnp.sum(both[8:16, :], axis=1, keepdims=True) / entries
    factor[...] = jnp.broadcast_to(jnp.sqrt(grad_mean) / jnp.sqrt(prod_mean + EPSILON), (8, LANES))
    squares.wait_send()


def store_kernel(prod, l_new, r_new, factor, update, l_out, r_out, scaled, sem):
    copies = [
        pltpu.make_async_copy(l_new, l_out, sem.at[0]),
        pltpu.make_async_copy(r_new, r_out, sem.at[1]),
        pltpu.make_async_copy(scaled, update, sem.at[2]),
    ]
    for copy in copies[:2]:
        copy.start()
    scaled[...] = (prod[...] * factor[0:1, 0:1]).astype(BF16)
    copies[2].start()
    for copy in copies:
        copy.wait()


def shards(grads, l_codes, l_scales, r_codes, r_scales, l_stats, r_stats):
    any_spec = pl.BlockSpec(memory_space=pl.ANY)
    vmem_spec = pl.BlockSpec(memory_space=pltpu.VMEM)
    wide = (ROWS, ORDER)
    dma = pltpu.SemaphoreType.DMA
    pieces = len(PIECES)
    outs = pl.pallas_call(
        kernel,
        name="shampoo",
        out_shape=(
            pltpu.VMEM(wide, F32),
            pltpu.VMEM(wide, F32),
            pltpu.VMEM(wide, F32),
            pltpu.VMEM((8, LANES), F32),
        ),
        in_specs=[any_spec] * 7,
        out_specs=(vmem_spec,) * 4,
        scratch_shapes=[
            pltpu.VMEM((RING, CHUNK, LANES), BF16),
            pltpu.VMEM((36, CHUNK, LANES), BF16),
            pltpu.VMEM((11, CHUNK, LANES), BF16),
            pltpu.VMEM((TEAM, RING, CHUNK, LANES), BF16),
            pltpu.VMEM(wide, jnp.int32),
            pltpu.VMEM(wide, jnp.int32),
            pltpu.VMEM((16, ROWS), F32),
            pltpu.VMEM((16, ROWS), F32),
            pltpu.VMEM((TEAM, ROWS, ROWS), BF16),
            pltpu.VMEM((TEAM, ROWS, ORDER), BF16),
            pltpu.VMEM(wide, F32),
            pltpu.VMEM(wide, BF16),
            pltpu.VMEM((4, 16, LANES), F32),
            dma((7,)), dma((pieces,)), dma((5 * pieces,)), dma((pieces,)), dma((5 * pieces,)),
            dma((pieces,)), dma((pieces,)), dma((2 * pieces,)), dma((2 * pieces,)),
            dma((3,)), dma((3,)), dma((1,)), dma((1,)),
        ],
        compiler_params=pltpu.CompilerParams(
            collective_id=0, has_side_effects=True, vmem_limit_bytes=40 * 2**20),
    )(*[pltpu.with_memory_space_constraint(a, pltpu.HBM) for a in (grads, l_codes, l_scales.T, r_codes, r_scales.T, l_stats, r_stats)])
    return pl.pallas_call(
        store_kernel,
        name="store",
        out_shape=(pltpu.HBM(wide, BF16), pltpu.HBM(wide, F32), pltpu.HBM(wide, F32)),
        in_specs=[vmem_spec] * 4,
        out_specs=(any_spec,) * 3,
        scratch_shapes=[pltpu.VMEM(wide, BF16), dma((3,))],
        compiler_params=pltpu.CompilerParams(vmem_limit_bytes=16 * 2**20),
    )(*outs)


def solution(mesh):
    return jax.shard_map(
        shards,
        mesh=mesh,
        in_specs=(
            P("fsdp", "blk", None),
            P("blk", None),
            P("blk", None),
            P("blk", None),
            P("blk", None),
            P("blk", None),
            P("blk", None),
        ),
        out_specs=(P("blk", None), P("blk", None), P("blk", None)),
        check_vma=False,
    )
```

```python
import functools

import jax
import jax.numpy as jnp
from jax import lax
from jax.experimental import pallas as pl
from jax.experimental.pallas import tpu as pltpu
from jax.sharding import PartitionSpec as P

BETA = 0.9
EPSILON = 1e-06
MESH = pl.DeviceIdType.MESH
F32 = jnp.float32
BF16 = jnp.bfloat16

ROWS = 256
ORDER = 1024
TEAM = 4
RING = 12
LANES = 128
CHUNK = 176
GROUP = 3 * CHUNK
PAIRS = 4

KEYS = (0, -3, -5, 6, 5, 3, -1, 1, -4, 4, -2, 2)
SLOT = {key: at for at, key in enumerate(KEYS[1:])}
SUM_WAIT = {-4: 0, 4: 1, 0: 2, -1: 3, 1: 4}
SPREAD_WAIT = {-1: 0, 1: 1, -4: 2, 4: 3, -2: 4, 2: 4, -3: 4, 3: 4, -5: 4, 5: 4, 6: 4}
PIECES = ((0, 80), (80, 96))
DIAGONAL = (2, 3, 5, 6)
LINKS = {1: (0, 1), 2: (1, 1), 4: (0, 4), 3: (4, -1), 5: (4, 1), 6: (4, 2)}


def tree(turn):
    links = {}
    for far, (near, step) in LINKS.items():
        if far == 6:
            links[6] = (-turn * near, turn * step)
        else:
            for s in (turn, -turn):
                links[-s * far] = (-s * near, s * step)
    return links


def depth(links, key):
    return 0 if key == 0 else 1 + depth(links, links[key][0])


def height(links, key):
    return max([1 + height(links, far) for far, (near, _) in links.items() if near == key], default=0)


def turn_of(piece):
    return 1 if piece % 2 == 0 else -1


def kernel(grads, l_codes, l_scales, r_codes, r_scales, l_stats, r_stats,
           prod, l_out, r_out, factor,
           x, acc, rbuf, gall, l_code_v, r_code_v, l_scale_v, r_scale_v,
           l_root, r_all, total, mixed, sq,
           load_sem, rs_send, rs_recv, ag_send, ag_recv, y_send, y_recv, c_send, c_recv,
           r_send, r_recv, s_send, s_recv):
    z = lax.axis_index("fsdp")
    blk = lax.axis_index("blk")
    member = lax.rem(blk, TEAM)
    base = blk - member
    m_y = lax.rem(member + 2, TEAM)
    m_c = member + 1 - 2 * lax.rem(member, 2)
    m_yc = lax.rem(m_c + 2, TEAM)

    def ring(step, which=None):
        return (lax.rem(z + step + RING, RING), blk if which is None else base + which)

    def mate(which):
        return (z, base + which)

    barrier = pltpu.get_barrier_semaphore()
    steps = sorted({abs(step) for _, step in LINKS.values()})
    partners = [ring(s * step) for step in reversed(steps) for s in (1, -1)] + [mate(m_y), mate(m_c), mate(m_yc)]
    cross = sorted({abs(LINKS[key][1]) for key in DIAGONAL})
    partners += [ring(s * step, m_y) for step in cross for s in (1, -1)]
    for partner in partners:
        pl.semaphore_signal(barrier, inc=1, device_id=partner, device_id_type=MESH)

    grad_loads = []
    for pair in range(PAIRS):
        for panel, row, rows, chunk, at in (
                (0, 0, 176, 0, 0), (0, 176, 80, 1, 0), (1, 0, 96, 1, 80), (1, 96, 160, 2, 0)):
            grad_loads.append(pltpu.make_async_copy(
                grads.at[0, pl.ds(row, rows), pl.ds((2 * pair + panel) * LANES, LANES)],
                x.at[3 * pair + chunk, pl.ds(at, rows)], load_sem.at[6]))
    other = [
        pltpu.make_async_copy(r_scales, r_scale_v, load_sem.at[0]),
        pltpu.make_async_copy(r_codes, r_code_v, load_sem.at[1]),
        pltpu.make_async_copy(l_scales, l_scale_v, load_sem.at[2]),
        pltpu.make_async_copy(l_codes, l_code_v, load_sem.at[3]),
        pltpu.make_async_copy(l_stats, l_out, load_sem.at[4]),
        pltpu.make_async_copy(r_stats, r_out, load_sem.at[5]),
    ]
    for copy in grad_loads + other:
        copy.start()

    for pair in range(PAIRS):
        x[3 * pair + 2, pl.ds(160, 16), :] = jnp.zeros((16, LANES), BF16)
    pl.semaphore_wait(barrier, len(partners))

    def owner(key):
        return lax.rem(z + key + RING, RING)

    def remote(src, dst, send, recv, target):
        return pltpu.make_async_remote_copy(
            src_ref=src, dst_ref=dst, send_sem=send, recv_sem=recv,
            device_id=target, device_id_type=MESH)

    sends = []

    def rs_copy(src, key, piece):
        near, step = tree(turn_of(piece))[key]
        ref = rbuf.at[SLOT[key], pl.ds(*PIECES[piece])]
        remote(src, ref, rs_send.at[piece], rs_recv.at[5 * piece + SUM_WAIT[near]], ring(-step)).start()

    def gathered(key, piece):
        links = tree(turn_of(piece))
        cut = pl.ds(*PIECES[piece])
        slots = sorted(SLOT[far] for far in links if links[far][0] == key)
        ref = rbuf.at[pl.ds(slots[0], len(slots)), cut]
        remote(ref, ref, rs_send.at[piece], rs_recv.at[5 * piece + SUM_WAIT[key]], ring(1)).wait_recv()
        result = x[owner(key), cut, :].astype(F32)
        for slot in slots:
            result = result + rbuf[slot, cut, :].astype(F32)
        return result.astype(BF16)

    pltpu.make_async_copy(grads.at[0], mixed, load_sem.at[6]).wait()
    for piece in range(len(PIECES)):
        links = tree(turn_of(piece))
        leaves = [key for key in links if height(links, key) == 0]
        for key in sorted(leaves, key=lambda key: (-depth(links, key), -abs(links[key][1]))):
            rs_copy(x.at[owner(key), pl.ds(*PIECES[piece])], key, piece)

    spread_group = lax.broadcasted_iota(jnp.int32, (48, ORDER), 0) % 16
    spread_column = lax.broadcasted_iota(jnp.int32, (48, ORDER), 1) // 64
    spread = jnp.where(spread_group == spread_column, 1.0, 0.0).astype(BF16)

    def dequantize(codes, scales):
        scaled = scales[...] * (1.0 / 15.0)
        first = scaled.astype(BF16)
        rest = scaled - first.astype(F32)
        second = rest.astype(BF16)
        third = (rest - second.astype(F32)).astype(BF16)
        terms = jnp.concatenate([first.astype(F32), second.astype(F32), third.astype(F32)], axis=0)
        wide = lax.dot_general(jnp.transpose(terms).astype(BF16), spread, (((1,), (0,)), ((), ())),
                               preferred_element_type=F32)
        return ((2.0 * codes[...].astype(F32) - 15.0) * wide).astype(BF16)

    for copy in other[:2]:
        copy.wait()
    r_all[member] = dequantize(r_code_v, r_scale_v)
    r_y = remote(r_all.at[member], r_all.at[member], r_send.at[0], r_recv.at[0], mate(m_y))
    r_c = remote(r_all.at[member], r_all.at[member], r_send.at[1], r_recv.at[1], mate(m_c))
    r_y.start()
    r_c.start()

    links = tree(1)
    for level in range(max(depth(links, key) for key in links), 0, -1):
        for piece in range(len(PIECES)):
            links = tree(turn_of(piece))
            nodes = [key for key in links if height(links, key) and depth(links, key) == level]
            for key in reversed(nodes):
                at = 6 * (level - 1) + nodes.index(key)
                cut = pl.ds(*PIECES[piece])
                acc[at, cut, :] = gathered(key, piece)
                rs_copy(acc.at[at, cut], key, piece)
        if level == 1:
            for copy in other[2:4]:
                copy.wait()
            left = dequantize(l_code_v, l_scale_v)
            for which in range(TEAM):
                l_root[which] = left[:, which * ROWS:(which + 1) * ROWS]

    def z_send(key, piece):
        links = tree(turn_of(piece))
        beyond = [far for far in links if links[far][0] == key]
        ref = gall.at[member, owner(key), pl.ds(*PIECES[piece])]
        for far in sorted(beyond, key=lambda far: (-height(links, far), abs(links[far][1]) * (1 if key else -1))):
            at = 5 * piece + SPREAD_WAIT[far]
            step = links[far][1]
            remote(ref, ref, ag_send.at[piece], ag_recv.at[at], ring(step)).start()
            if abs(far) in DIAGONAL:
                remote(ref, ref, y_send.at[piece], y_recv.at[piece], ring(step, m_y)).start()

    def z_wait(key, piece):
        at = 5 * piece + SPREAD_WAIT[key]
        count = sum(1 for other_key in SPREAD_WAIT if SPREAD_WAIT[other_key] == SPREAD_WAIT[key])
        ref = gall.at[member, pl.ds(0, count), pl.ds(*PIECES[piece])]
        remote(ref, ref, ag_send.at[piece], ag_recv.at[at], ring(1)).wait_recv()

    def y_forward(key, piece):
        ref = gall.at[member, owner(key), pl.ds(*PIECES[piece])]
        remote(ref, ref, y_send.at[piece], y_recv.at[piece], mate(m_y)).start()

    def y_wait(piece):
        ref = gall.at[m_y, :, pl.ds(*PIECES[piece])]
        remote(ref, ref, y_send.at[piece], y_recv.at[piece], mate(m_y)).wait_recv()

    def c_copy(which, piece, set_at):
        at = piece * 2 + set_at
        ref = gall.at[which, :, pl.ds(*PIECES[piece])]
        return remote(ref, ref, c_send.at[at], c_recv.at[at], mate(m_c))

    def c_forward(which, piece, set_at):
        copy = c_copy(which, piece, set_at)
        copy.start()
        sends.append(copy)

    for piece in range(len(PIECES)):
        gall[member, z, pl.ds(*PIECES[piece]), :] = gathered(0, piece)
        z_send(0, piece)
        y_forward(0, piece)
    links = tree(1)
    levels = max(depth(links, key) for key in links)
    for level in range(1, levels + 1):
        for piece in range(len(PIECES)):
            links = tree(turn_of(piece))
            here = [key for key in links if depth(links, key) == level and abs(key) not in DIAGONAL]
            for key in sorted(here, key=lambda key: (-height(links, key), abs(links[key][1]))):
                z_wait(key, piece)
                z_send(key, piece)
                y_forward(key, piece)
            if level == levels:
                z_wait(6, piece)
                c_forward(member, piece, 0)
                y_wait(piece)
                c_forward(m_y, piece, 1)
        if level == 1:
            remote(r_all.at[m_y], r_all.at[m_y], r_send.at[0], r_recv.at[0], mate(m_y)).wait_recv()
            r_yc = remote(r_all.at[m_y], r_all.at[m_y], r_send.at[2], r_recv.at[2], mate(m_c))
            r_yc.start()

    def panel_pair(which, pair):
        both = gall[which, pl.ds(3 * pair, 3)].reshape(GROUP, LANES)
        return jnp.concatenate([both[:ROWS], both[ROWS:2 * ROWS]], axis=1)

    def rows_of(which):
        return jnp.concatenate([panel_pair(which, pair) for pair in range(PAIRS)], axis=1)

    def mix(which, first=False):
        part = jnp.dot(l_root[which], rows_of(which), preferred_element_type=F32)
        return part if first else total[...] + part

    scale = (1.0 - BETA) / ORDER

    def grams(which, first=False):
        cut = pl.ds(pl.multiple_of(which * ROWS, ROWS), ROWS)
        left = lax.dot_general(rows_of(member), rows_of(which), (((1,), (1,)), ((), ())), preferred_element_type=F32)
        l_out[:, cut] = BETA * l_out[:, cut] + scale * left
        right = jnp.dot(jnp.transpose(panel_pair(which, member)), rows_of(which), preferred_element_type=F32)
        r_out[...] = (BETA * r_out[...] if first else r_out[...]) + scale * right

    total[...] = mix(member, True)
    total[...] = mix(m_y)
    grad_square = jnp.sum(jnp.square(rows_of(member).astype(F32)), axis=0, keepdims=True)
    grad_square = sum(grad_square[:, at * LANES:(at + 1) * LANES] for at in range(8))
    remote(r_all.at[m_c], r_all.at[m_c], r_send.at[1], r_recv.at[1], mate(m_c)).wait_recv()
    remote(r_all.at[m_yc], r_all.at[m_yc], r_send.at[2], r_recv.at[2], mate(m_c)).wait_recv()
    for piece in range(len(PIECES)):
        c_copy(m_c, piece, 0).wait_recv()
    total[...] = mix(m_c)
    for piece in range(len(PIECES)):
        c_copy(m_yc, piece, 1).wait_recv()
    mixed[...] = mix(m_yc).astype(BF16)
    square = jnp.zeros((ROWS, ROWS), F32)
    for pair in range(PAIRS):
        right = jnp.concatenate([r_all[which, :, pl.ds(pair * ROWS, ROWS)] for which in range(TEAM)], axis=0)
        part = jnp.dot(mixed[...], right, preferred_element_type=F32)
        prod[:, pl.ds(pair * ROWS, ROWS)] = part
        square = square + part * part
    prod_square = jnp.sum(square, axis=0, keepdims=True)
    prod_square = prod_square[:, :LANES] + prod_square[:, LANES:]
    sq[3] = jnp.concatenate(
        [jnp.broadcast_to(grad_square, (8, LANES)), jnp.broadcast_to(prod_square, (8, LANES))], axis=0)
    for at, which in enumerate((m_y, m_c, m_yc)):
        remote(sq.at[3], sq.at[at], s_send.at[0], s_recv.at[0], mate(which)).start()
    for copy in other[4:]:
        copy.wait()
    grams(member, True)
    for which in (m_y, m_c, m_yc):
        grams(which)

    for copy in sends + [r_y, r_c, r_yc]:
        copy.wait_send()
    for piece in range(len(PIECES)):
        cut = pl.ds(*PIECES[piece])
        ref = rbuf.at[:, cut]
        remote(ref, ref, rs_send.at[piece], rs_recv.at[5 * piece], ring(1)).wait_send()
        ref = gall.at[member, pl.ds(0, 11), cut]
        remote(ref, ref, ag_send.at[piece], ag_recv.at[5 * piece], ring(1)).wait_send()
        ref = gall.at[member, :, cut]
        remote(ref, ref, y_send.at[piece], y_recv.at[piece], mate(m_y)).wait_send()
    squares = remote(sq.at[pl.ds(0, 3)], sq.at[pl.ds(0, 3)], s_send.at[0], s_recv.at[0], mate(m_y))
    squares.wait_recv()
    both = sq[0] + sq[1] + sq[2] + sq[3]
    entries = float(ORDER * ORDER)
    grad_mean = jnp.sum(both[0:8, :], axis=1, keepdims=True) / entries
    prod_mean = jnp.sum(both[8:16, :], axis=1, keepdims=True) / entries
    factor[...] = jnp.broadcast_to(jnp.sqrt(grad_mean) / jnp.sqrt(prod_mean + EPSILON), (8, LANES))
    squares.wait_send()


def store_kernel(prod, l_new, r_new, factor, update, l_out, r_out, scaled, sem):
    copies = [
        pltpu.make_async_copy(l_new, l_out, sem.at[0]),
        pltpu.make_async_copy(r_new, r_out, sem.at[1]),
        pltpu.make_async_copy(scaled, update, sem.at[2]),
    ]
    for copy in copies[:2]:
        copy.start()
    scaled[...] = (prod[...] * factor[0:1, 0:1]).astype(BF16)
    copies[2].start()
    for copy in copies:
        copy.wait()


def shards(grads, l_codes, l_scales, r_codes, r_scales, l_stats, r_stats):
    any_spec = pl.BlockSpec(memory_space=pl.ANY)
    vmem_spec = pl.BlockSpec(memory_space=pltpu.VMEM)
    wide = (ROWS, ORDER)
    dma = pltpu.SemaphoreType.DMA
    pieces = len(PIECES)
    outs = pl.pallas_call(
        kernel,
        name="shampoo",
        out_shape=(
            pltpu.VMEM(wide, F32),
            pltpu.VMEM(wide, F32),
            pltpu.VMEM(wide, F32),
            pltpu.VMEM((8, LANES), F32),
        ),
        in_specs=[any_spec] * 7,
        out_specs=(vmem_spec,) * 4,
        scratch_shapes=[
            pltpu.VMEM((RING, CHUNK, LANES), BF16),
            pltpu.VMEM((36, CHUNK, LANES), BF16),
            pltpu.VMEM((11, CHUNK, LANES), BF16),
            pltpu.VMEM((TEAM, RING, CHUNK, LANES), BF16),
            pltpu.VMEM(wide, jnp.int32),
            pltpu.VMEM(wide, jnp.int32),
            pltpu.VMEM((16, ROWS), F32),
            pltpu.VMEM((16, ROWS), F32),
            pltpu.VMEM((TEAM, ROWS, ROWS), BF16),
            pltpu.VMEM((TEAM, ROWS, ORDER), BF16),
            pltpu.VMEM(wide, F32),
            pltpu.VMEM(wide, BF16),
            pltpu.VMEM((4, 16, LANES), F32),
            dma((7,)), dma((pieces,)), dma((5 * pieces,)), dma((pieces,)), dma((5 * pieces,)),
            dma((pieces,)), dma((pieces,)), dma((2 * pieces,)), dma((2 * pieces,)),
            dma((3,)), dma((3,)), dma((1,)), dma((1,)),
        ],
        compiler_params=pltpu.CompilerParams(
            collective_id=0, has_side_effects=True, vmem_limit_bytes=40 * 2**20),
    )(*[pltpu.with_memory_space_constraint(a, pltpu.HBM) for a in (grads, l_codes, l_scales.T, r_codes, r_scales.T, l_stats, r_stats)])
    return pl.pallas_call(
        store_kernel,
        name="store",
        out_shape=(pltpu.HBM(wide, BF16), pltpu.HBM(wide, F32), pltpu.HBM(wide, F32)),
        in_specs=[vmem_spec] * 4,
        out_specs=(any_spec,) * 3,
        scratch_shapes=[pltpu.VMEM(wide, BF16), dma((3,))],
        compiler_params=pltpu.CompilerParams(vmem_limit_bytes=16 * 2**20),
    )(*outs)


def solution(mesh):
    return jax.shard_map(
        shards,
        mesh=mesh,
        in_specs=(
            P("fsdp", "blk", None),
            P("blk", None),
            P("blk", None),
            P("blk", None),
            P("blk", None),
            P("blk", None),
            P("blk", None),
        ),
        out_specs=(P("blk", None), P("blk", None), P("blk", None)),
        check_vma=False,
    )
```
